128 devices in a mesh: cand: 4 (over y_lo, core), ctx: 32 (over z, y_hi, x).
Axes of the slice: x: 4, y: 4 (y_hi: 2, y_lo: 2; y = y_hi * 2 + y_lo), z: 4, core: 2. Of those that a mesh axis runs over, the one named last changes fastest.
Arguments:
- history: bfloat16 [8, 65536, 256], P(None, 'ctx'), may hold values from -6 to 6
- candidates: bfloat16 [8, 2048, 256], P(None, 'cand'), may hold values from -70 to 70
- short_hist: bfloat16 [8, 256, 256], replicated, may hold values from -6 to 6
- lengths: int32 [8], replicated, may hold values from 8192 to 65536, as said below
- pad_mask: int32 [8, 65536], P(None, 'ctx'), may hold values 0 or 1
- short_mask: int32 [8, 256], replicated, may hold values 0 or 1
- query_gain: float32 [256], replicated, may hold values from 0.5 to 2
- value_weight: bfloat16 [256, 256], replicated, may hold values from -0.375 to 0.375
- head_weight: bfloat16 [256, 256], replicated, may hold values from -0.375 to 0.375
- head_vector: float32 [256], replicated, may hold values from -1.5 to 1.5
- pair_weight: float32 [256, 128], replicated, may hold values from -0.375 to 0.375
- event_weight: float32 [256, 128], replicated, may hold values from -0.375 to 0.375
- scoring_bias: float32 [128], replicated, may hold values from -3 to 3
- weigher: float32 [128], replicated, may hold values from -0.5 to 0.5
- pooling_weight: float32 [256, 256], replicated, may hold values from -0.046875 to 0.046875
- itemwise_weight: float32 [256, 256], replicated, may hold values from -0.375 to 0.375
- hidden_bias: float32 [256], replicated, may hold values from -3 to 3
- output_vector: float32 [256], replicated, may hold values from -1.5 to 1.5
Outputs:
- teacher_logits: float32 [8, 2048], P(None, ('cand', 'ctx'))
- pair_grad: float32 [256, 128], replicated
- event_grad: float32 [256, 128], replicated
- scoring_grad: float32 [128], replicated
- weigher_grad: float32 [128], replicated
- pooling_grad: float32 [256, 256], replicated
- itemwise_grad: float32 [256, 256], replicated
- hidden_grad: float32 [256], replicated
- output_grad: float32 [256], replicated
The draws below stay inside these ranges and needn't reach their ends.
Inputs may be any that keep to these rules, and one draw needn't show every extreme that they name: `lengths`: valid history events of each user, counted from the first position.
All inputs are finite; a program needn't handle non-finite values. No bound on the sum of `pad_mask` on one device may be relied on, other than what follows from the above.
Results may differ from the reference program's by a relative error of at most 0.029.
Values sent between devices are 32-bit elements; how exact they have to be, the bound alone decides.
A program may use at most 384 MiB of HBM per device.

```python
import math
import jax
import jax.numpy as jnp
from jax import lax

USERS = 8
CANDS = 2048
HIST_DEV = 2048
HIST = 65536
SHORT = 256
EMBED = 256
HEAD_H = 256
SCORE_H = 128
MLP_H = 256


def base_events(key):
    return jnp.clip(jax.random.normal(key, (USERS, HIST, EMBED), jnp.float32), -4.5, 4.5)


def draw_history(key, part):
    events = base_events(key)
    return events.astype(jnp.bfloat16)


def draw_candidates(key, part):
    key = jax.random.fold_in(key, 9)
    rows = jnp.clip(jax.random.normal(key, (USERS, CANDS, EMBED), jnp.float32), -4.5, 4.5)
    return rows.astype(jnp.bfloat16)


def draw_lengths(key, part):
    key = jax.random.fold_in(key, 5)
    drawn = jax.random.randint(key, (USERS,), HIST // 8, HIST + 1, dtype=jnp.int32)
    places = jnp.arange(USERS, dtype=jnp.int32)
    anchored = jnp.where(places == 0, HIST, HIST // 8).astype(jnp.int32)
    return jnp.where(places < 2, anchored, drawn).astype(jnp.int32)


def touch_ends(result, own_key, low, top_value):
    place = [jax.random.randint(jax.random.fold_in(own_key, axis), (), 0, length) for axis, length in enumerate(result.shape)]
    main_axis = result.shape.index(max(result.shape))
    beside = place[:main_axis] + [(place[main_axis] + 1) % result.shape[main_axis]] + place[main_axis + 1:]
    return result.at[tuple(place)].set(low).at[tuple(beside)].set(top_value)


def gaussian(key, shape, deviation, bound, held_as=jnp.bfloat16):
    return jnp.clip(deviation * jax.random.normal(key, shape, jnp.float32), -bound, bound).astype(held_as)


def setup_inputs(seed: int = 0) -> dict:
    splits = jax.random.split(jax.random.key(seed), 19)
    history = draw_history(jax.random.fold_in(splits[18], 71), 0)
    candidates = draw_candidates(jax.random.fold_in(splits[18], 71), 0)
    short_hist = gaussian(splits[2], (USERS, SHORT, EMBED), 1.0, 6.0)
    lengths = draw_lengths(jax.random.fold_in(splits[18], 71), 0)
    pad_mask = touch_ends((jax.random.randint(splits[4], (USERS, HIST), 0, 8) < 7).astype(jnp.int32), jax.random.fold_in(splits[4], 1), 0, 1)
    short_mask = touch_ends((jax.random.randint(splits[5], (USERS, SHORT), 0, 8) < 7).astype(jnp.int32), jax.random.fold_in(splits[5], 1), 0, 1)
    query_gain = jnp.clip(jnp.exp(jax.random.uniform(splits[6], (EMBED,), jnp.float32, math.log(0.5), math.log(2.0))), 0.5, 2.0)
    value_weight = gaussian(splits[7], (EMBED, EMBED), EMBED ** -0.5, 0.375)
    head_weight = gaussian(splits[8], (EMBED, HEAD_H), EMBED ** -0.5, 0.375)
    head_vector = gaussian(splits[9], (HEAD_H,), (HEAD_H // 16) ** -0.5, 1.5, jnp.float32)
    pair_weight = gaussian(splits[10], (EMBED, SCORE_H), EMBED ** -0.5, 0.375, jnp.float32)
    event_weight = gaussian(splits[11], (EMBED, SCORE_H), EMBED ** -0.5, 0.375, jnp.float32)
    scoring_bias = gaussian(splits[12], (SCORE_H,), 0.5, 3.0, jnp.float32)
    weigher = gaussian(splits[13], (SCORE_H,), SCORE_H ** -0.5, 0.5, jnp.float32)
    pooling_weight = gaussian(splits[14], (EMBED, MLP_H), (EMBED * SHORT // 4) ** -0.5, 0.046875, jnp.float32)
    itemwise_weight = gaussian(splits[15], (EMBED, MLP_H), EMBED ** -0.5, 0.375, jnp.float32)
    hidden_bias = gaussian(splits[16], (MLP_H,), 0.5, 3.0, jnp.float32)
    output_vector = gaussian(splits[17], (MLP_H,), (MLP_H // 16) ** -0.5, 1.5, jnp.float32)
    return {"history": history, "candidates": candidates, "short_hist": short_hist, "lengths": lengths, "pad_mask": pad_mask, "short_mask": short_mask, "query_gain": query_gain, "value_weight": value_weight, "head_weight": head_weight, "head_vector": head_vector, "pair_weight": pair_weight, "event_weight": event_weight, "scoring_bias": scoring_bias, "weigher": weigher, "pooling_weight": pooling_weight, "itemwise_weight": itemwise_weight, "hidden_bias": hidden_bias, "output_vector": output_vector}


NEG_FILL = -1e+30
SOFT_CAP = 10.0
HIGHEST = lax.Precision.HIGHEST

def capped(logits):
    return SOFT_CAP * jnp.tanh(logits / SOFT_CAP)

def combine_parts(first, second):
    highest = jnp.maximum(first[0], second[0])
    first_factor = jnp.exp(first[0] - highest)
    second_factor = jnp.exp(second[0] - highest)
    totals = first[1] * first_factor + second[1] * second_factor
    weighted = first[2] * first_factor[..., None] + second[2] * second_factor[..., None]
    return (highest, totals, weighted)

def teacher_head(pooled, cand_rows, head_weight, head_vector):
    normed = pooled * lax.rsqrt(lax.optimization_barrier(jnp.mean(pooled * pooled, axis=-1, keepdims=True)) + 1e-06)
    mixed = (normed * cand_rows.astype(jnp.float32)).astype(jnp.bfloat16)
    hidden = jax.nn.gelu(jnp.einsum('ure,eh->urh', mixed.astype(jnp.float32), head_weight.astype(jnp.float32)))
    return capped(lax.optimization_barrier(jnp.sum(hidden * head_vector, axis=-1)))

def student(params, short_f, short_ok, cand_f):
    pair_weight, event_weight, scoring_bias, weigher, pooling_weight, itemwise_weight, hidden_bias, output_vector = params
    event_part = jnp.einsum('use,ea->usa', short_f, event_weight, precision=HIGHEST)
    pairs = cand_f[:, :, None, :] * short_f[:, None, :, :]
    activation = jax.nn.relu(jnp.einsum('urse,ea->ursa', pairs, pair_weight, precision=HIGHEST) + event_part[:, None] + scoring_bias)
    attention = jnp.einsum('ursa,a->urs', activation, weigher, precision=HIGHEST)
    attention = jnp.where(short_ok[:, None, :], attention, 0.0)
    interest = jnp.einsum('urs,use->ure', attention, short_f, precision=HIGHEST)
    hidden = jax.nn.gelu(jnp.einsum('ure,eh->urh', interest, pooling_weight, precision=HIGHEST) + jnp.einsum('ure,eh->urh', cand_f, itemwise_weight, precision=HIGHEST) + hidden_bias)
    return capped(jnp.einsum('urh,h->ur', hidden, output_vector, precision=HIGHEST))

def reference(history, candidates, short_hist, lengths, pad_mask, short_mask, query_gain, value_weight, head_weight, head_vector, pair_weight, event_weight, scoring_bias, weigher, pooling_weight, itemwise_weight, hidden_bias, output_vector):
    positions = jnp.arange(HIST, dtype=jnp.int32)
    event_ok = (positions[None, :] < lengths[:, None]) & ((pad_mask == 1) | (positions[None, :] == 0))
    query = (candidates.astype(jnp.float32) * query_gain).astype(jnp.bfloat16)
    inverse_root = 1.0 / math.sqrt(EMBED)

    def teacher_user(operands):
        hist_user, query_user, ok_user = operands

        def block_step(carry, index):
            start = (index * HIST_DEV).astype(jnp.int32)
            keys = lax.dynamic_slice_in_dim(hist_user, start, HIST_DEV, 0)
            ok_block = lax.dynamic_slice_in_dim(ok_user, start, HIST_DEV, 0)
            values = jnp.dot(keys, value_weight, preferred_element_type=jnp.float32).astype(jnp.bfloat16)
            scores = lax.dot_general(query_user, keys, (((1,), (1,)), ((), ())), preferred_element_type=jnp.float32) * inverse_root
            block_max = lax.optimization_barrier(jnp.max(jnp.where(ok_block[None, :], scores, NEG_FILL), axis=1))
            block_exp = jnp.where(ok_block[None, :], jnp.exp(scores - block_max[:, None]), 0.0)
            block_total = lax.optimization_barrier(jnp.sum(block_exp, axis=1))
            block_value = jnp.dot(block_exp.astype(jnp.bfloat16), values, preferred_element_type=jnp.float32)
            return (combine_parts(carry, (block_max, block_total, block_value)), None)
        start_carry = (jnp.full((CANDS,), NEG_FILL, jnp.float32), jnp.zeros((CANDS,), jnp.float32), jnp.zeros((CANDS, EMBED), jnp.float32))
        merged, _ = lax.scan(block_step, start_carry, jnp.arange(HIST // HIST_DEV, dtype=jnp.int32))
        return merged[2] / merged[1][:, None]
    pooled = lax.map(teacher_user, (history, query, event_ok))
    teacher_logits = teacher_head(pooled, candidates, head_weight, head_vector)
    short_pos = jnp.arange(SHORT, dtype=jnp.int32)
    short_ok = (short_mask == 1) | (short_pos[None, :] == 0)
    short_f = short_hist.astype(jnp.float32)
    cand_f = candidates.astype(jnp.float32)
    params = (pair_weight, event_weight, scoring_bias, weigher, pooling_weight, itemwise_weight, hidden_bias, output_vector)
    block_count = CANDS // 64

    def all_logits(param_set):
        blocks = cand_f.reshape(USERS, block_count, 64, EMBED).transpose(1, 0, 2, 3)
        piece = jax.checkpoint(lambda rows: student(param_set, short_f, short_ok, rows))
        outputs = lax.map(piece, blocks)
        return outputs.transpose(1, 0, 2).reshape(USERS, CANDS)
    student_logits, pull = jax.vjp(all_logits, params)
    teacher_exp = jnp.exp(teacher_logits)
    student_exp = jnp.exp(student_logits)
    teacher_probs = teacher_exp / lax.optimization_barrier(jnp.sum(teacher_exp, axis=1, keepdims=True))
    student_probs = student_exp / lax.optimization_barrier(jnp.sum(student_exp, axis=1, keepdims=True))
    logit_grad = math.sqrt(CANDS / USERS) * (student_probs - teacher_probs)
    grads = pull(logit_grad)[0]
    return (teacher_logits, grads[0], grads[1], grads[2], grads[3], grads[4], grads[5], grads[6], grads[7])
```

```python
import functools
import math

import jax
import jax.numpy as jnp
from jax import lax
from jax.experimental import pallas as pl
from jax.experimental.pallas import tpu as pltpu
from jax.sharding import PartitionSpec as P

NEG_FILL = -1e30
NEG_CLAMP = -1e29
SOFT_CAP = 10.0
HIGHEST = lax.Precision.HIGHEST
F32 = jnp.float32
BF16 = jnp.bfloat16
MESH = pl.DeviceIdType.MESH

USERS = 8
CAND_DEV = 512
EVENTS = 2048
WIDTH = 256
SHORT = 256
SCORE_H = 128
OWN = 16
BLOCKS = 32
OWN_ALL = USERS * OWN
CGROUP = 4
DELAY = (3, 5, 6, 7, 8)
GELU_K = math.sqrt(2.0 / math.pi)
GELU_C = 0.044715


def dot(a, b, ca=1, cb=0, precision=None):
    return lax.dot_general(
        a, b, (((ca,), (cb,)), ((), ())), precision=precision, preferred_element_type=F32
    )


def gelu(p):
    return 0.5 * p * (1.0 + jnp.tanh(GELU_K * (p + GELU_C * p * p * p)))


def diag_row(col, n=128):
    lane = lax.broadcasted_iota(jnp.int32, (n, n), 1)
    sub = lax.broadcasted_iota(jnp.int32, (n, n), 0)
    return jnp.sum(jnp.where(lane == sub, jnp.broadcast_to(col, (n, n)), 0.0), axis=0, keepdims=True)


def to_column(row):
    return jnp.transpose(jnp.broadcast_to(row, (128, 128)))


def main_kernel(
    lengths,
    history,
    candidates,
    short,
    pad_mask,
    short_mask,
    query_gain,
    value_weight,
    head_weight,
    head_vector,
    pair_weight,
    event_weight,
    scoring_bias,
    weigher,
    pooling_weight,
    itemwise_weight,
    hidden_bias,
    output_vector,
    logits_out,
    grads_out,
    small_out,
    hist,
    qs,
    scores,
    probs,
    inv_col,
    lse_col,
    acc,
    lse,
    rv0,
    rv1,
    rv2,
    rv3,
    rv4,
    rl,
    oc,
    pw_t,
    ew_t,
    w_full,
    b_full,
    wb,
    pre,
    att,
    interest,
    datt,
    pg,
    mtot,
    msum,
    eg,
    rows_t,
    dh,
    mlp,
    st1,
    st2,
    sm1,
    sm2,
    gb,
    r0,
    r1,
    r2,
    hist_sem,
    rs_vs,
    rs_vr,
    rs_ls,
    rs_lr,
    st1_s,
    st1_r,
    st2_s,
    st2_r,
    sm1_s,
    sm1_r,
    sm2_s,
    sm2_r,
    a0_s,
    a0_r,
    a1_s,
    a1_r,
    a2_s,
    a2_r,
    a3_s,
    a3_r,
    a4_s,
    a4_r,
):
    rv = (rv0, rv1, rv2, rv3, rv4)
    cand = lax.axis_index("cand")
    ctx = lax.axis_index("ctx")
    x = ctx % 4
    y_hi = (ctx // 4) % 2
    z = ctx // 8
    y_lo = cand // 2
    core = cand % 2
    y = y_hi * 2 + y_lo
    place8 = y_hi * 4 + cand
    place16 = z * 4 + x

    def peer8(k):
        return (k % 4, z * 8 + (k // 4) * 4 + x)

    def peer16(k):
        return (cand, (k // 4) * 8 + y_hi * 4 + k % 4)

    def peer_y(k):
        return ((k % 2) * 2 + core, z * 8 + (k // 2) * 4 + x)

    sibling = (y_lo * 2 + 1 - core, ctx)

    def hist_copy(u):
        return pltpu.make_async_copy(history.at[u], hist.at[u], hist_sem.at[u])

    barrier = pltpu.get_barrier_semaphore()
    for d in range(1, 8):
        pl.semaphore_signal(barrier, inc=1, device_id=peer8((place8 + d) % 8), device_id_type=MESH)
    for d in range(1, 16):
        pl.semaphore_signal(
            barrier, inc=1, device_id=peer16((place16 + d) % 16), device_id_type=MESH
        )
    for u in range(USERS):
        hist_copy(u).start()

    pw_t[...] = jnp.transpose(pair_weight[...])
    ew_t[...] = jnp.transpose(event_weight[...])
    wc = to_column(weigher[...])
    bc = to_column(scoring_bias[...])
    w_full[:, :128] = wc
    w_full[:, 128:] = wc
    b_full[:, :128] = bc
    b_full[:, 128:] = bc
    for u in range(USERS):
        oc[u] = candidates[u, pl.ds(pl.multiple_of(ctx * OWN, OWN), OWN), :].astype(F32)
    pg[...] = jnp.zeros_like(pg)
    mtot[...] = jnp.zeros_like(mtot)
    eg[...] = jnp.zeros_like(eg)

    stride1 = 1 + 7 * core
    stride2 = 8 - 7 * core
    c1 = (ctx // stride1) % 4
    c2 = (ctx // stride2) % 4

    def bits_of(c):
        low, high = c % 2, c // 2
        return low + high - 2 * low * high, high

    def rs_plan(k, u):
        q = u % 2
        a1, b1 = bits_of(c1)
        a2, b2 = bits_of(c2)
        bits = (a1 + q * (b1 - a1), b1 + q * (a1 - b1), a2 + q * (b2 - a2), b2 + q * (a2 - b2), y_hi)
        start = 0
        for j in range(k):
            start = start + bits[j] * (16 >> j)
        n = 16 >> k
        keep = start + bits[k] * n
        send = start + (1 - bits[k]) * n
        if k == 4:
            partner = ctx + (1 - 2 * y_hi) * 4
        else:
            c, stride = (c1, stride1) if k < 2 else (c2, stride2)
            pa = c + 1 - 2 * (c % 2)
            pb = 3 - c
            pc = pa + q * (pb - pa) if k % 2 == 0 else pb + q * (pa - pb)
            partner = ctx + (pc - c) * stride
        return (cand, partner), keep, send

    def rs_copies(k, u):
        device, _, send = rs_plan(k, u)
        n = 16 >> k
        value = pltpu.make_async_remote_copy(
            src_ref=acc.at[u, pl.ds(send, n)],
            dst_ref=rv[k].at[u],
            send_sem=rs_vs.at[k, u],
            recv_sem=rs_vr.at[k, u],
            device_id=device,
            device_id_type=MESH,
        )
        if k == 0:
            src, dst = lse.at[k, u, pl.ds(send // 8, 2)], rl.at[u, pl.ds(0, 2)]
        else:
            src, dst = lse.at[k, u, pl.ds(send // 8, 1)], rl.at[u, pl.ds(1 + k, 1)]
        weight = pltpu.make_async_remote_copy(
            src_ref=src,
            dst_ref=dst,
            send_sem=rs_ls.at[k, u],
            recv_sem=rs_lr.at[k, u],
            device_id=device,
            device_id_type=MESH,
        )
        return value, weight

    def rs_send(k, u):
        for copy in rs_copies(k, u):
            copy.start()

    def rs_merge(k, u):
        for copy in rs_copies(k, u):
            copy.wait()
        _, keep, _ = rs_plan(k, u)
        n = 16 >> k
        rows = 2 if k == 0 else 1
        per_row = min(n, 8)
        for r in range(rows):
            row = keep // 8 + r
            mine = lse[k, u, row]
            other = rl[u, (r if k == 0 else 1 + k)]
            top = jnp.maximum(mine, other)
            e_mine = jnp.exp(mine - top)
            e_other = jnp.exp(other - top)
            total = e_mine + e_other
            share = e_other / total
            if k < 4:
                lse[k + 1, u, row] = top + jnp.log(total)
            share16 = jnp.concatenate([share, share], axis=0)
            lane = lax.broadcasted_iota(jnp.int32, (16, 128), 1)
            sub = lax.broadcasted_iota(jnp.int32, (16, 128), 0)
            for b in range(per_row):
                at = keep + r * 8 + b
                off = (at % 8) * 16
                col = jnp.sum(
                    jnp.where(lane - sub == off, share16, 0.0), axis=1, keepdims=True
                )
                own = acc[u, at]
                got = rv[k][u, r * 8 + b]
                acc[u, at] = own + col * (got - own)

    def teacher_user(u):
        q = u % 2
        gain = query_gain[...] * (1.0 / 16.0)
        for pos in range(BLOCKS):
            p4, p3, p2, p1, p0 = ((pos >> s) & 1 for s in (4, 3, 2, 1, 0))
            first = 2 * (p3 + q * (p4 - p3)) + (p4 ^ p3)
            second = 2 * (p1 + q * (p2 - p1)) + (p2 ^ p1)
            block = first * stride1 + second * stride2 + p0 * 4
            rows = candidates[u, pl.ds(pl.multiple_of(block * 16, 16), 16), :]
            qs[pos * 16 : pos * 16 + 16, :] = (rows.astype(F32) * gain).astype(BF16)
        spot = lax.broadcasted_iota(jnp.int32, (1, EVENTS), 1) + ctx * EVENTS
        ok = (spot < lengths[u]) & ((pad_mask[pl.ds(u, 1), :] == 1) | (spot == 0))
        bias = jnp.where(ok, 0.0, NEG_FILL)
        hist_copy(u).wait()
        for t in range(4):
            cols = slice(t * 512, t * 512 + 512)
            scores[:, cols] = dot(qs[...], hist[u, cols, :], 1, 1) + bias[:, cols]

        def soft(r, carry):
            rows = pl.ds(pl.multiple_of(r * 32, 32), 32)
            s = scores[rows, :]
            m = jnp.maximum(jnp.max(s, axis=1, keepdims=True), NEG_CLAMP)
            e = jnp.exp(s - m)
            total = jnp.sum(e, axis=1, keepdims=True)
            probs[rows, :] = e.astype(BF16)
            some = total > 0.0
            safe = jnp.where(some, total, 1.0)
            lse_col[rows, :] = jnp.broadcast_to(
                jnp.where(some, m + jnp.log(safe), NEG_FILL), (32, 128)
            )
            inv_col[rows, :] = jnp.broadcast_to(1.0 / safe, (32, 128))
            return carry

        lax.fori_loop(0, 16, soft, 0)
        lane = lax.broadcasted_iota(jnp.int32, (128, 128), 1)
        sub = lax.broadcasted_iota(jnp.int32, (128, 128), 0)
        for g in range(4):
            rows = slice(g * 128, g * 128 + 128)
            row = jnp.sum(jnp.where(lane == sub, lse_col[rows, :], 0.0), axis=0, keepdims=True)
            lse[0, u, g] = jnp.broadcast_to(row, (8, 128))
        for t in range(2):
            rows = slice(t * 256, t * 256 + 256)
            out = dot(probs[rows, :], hist[u])
            inv = inv_col[rows, :]
            acc[u, t * 16 : t * 16 + 16, :, :128] = (out[:, :128] * inv).reshape(16, 16, 128)
            acc[u, t * 16 : t * 16 + 16, :, 128:] = (out[:, 128:] * inv).reshape(16, 16, 128)

    def short_ok(u):
        spot = lax.broadcasted_iota(jnp.int32, (1, SHORT), 1)
        return (short_mask[pl.ds(u, 1), :] == 1) | (spot == 0)

    def student_user(u):
        def group(cg, carry):
            for j in range(CGROUP):
                c = cg * CGROUP + j
                w = pw_t[...] * oc[u, pl.ds(c, 1), :] + ew_t[...]
                high = w.astype(BF16)
                wb[0, j * 128 : j * 128 + 128, :] = high
                wb[1, j * 128 : j * 128 + 128, :] = (w - high.astype(F32)).astype(BF16)
            p = dot(wb[0], short[u], 1, 1) + dot(wb[1], short[u], 1, 1)
            for j in range(CGROUP):
                c = cg * CGROUP + j
                pj = p[j * 128 : j * 128 + 128, :] + b_full[...]
                pre[u, c] = pj
                att[u, pl.ds(c, 1), :] = jnp.sum(
                    jnp.maximum(pj, 0.0) * w_full[...], axis=0, keepdims=True
                )
            return carry

        lax.fori_loop(0, OWN // CGROUP, group, 0)
        weights = jnp.where(short_ok(u), att[u], 0.0)
        interest[u] = dot(weights, short[u].astype(F32), 1, 0, HIGHEST)

    pl.semaphore_wait(barrier, 22)

    def teacher_slot(i, carry):
        teacher_user(i)
        rs_send(0, i)
        for k in reversed(range(5)):

            @pl.when(i >= DELAY[k])
            def _(k=k):
                rs_merge(k, i - DELAY[k])
                if k < 4:
                    rs_send(k + 1, i - DELAY[k])

        return carry

    lax.fori_loop(0, USERS, teacher_slot, 0)

    def student_slot(i, carry):
        student_user(i - USERS)
        for k in reversed(range(5)):

            @pl.when(i - DELAY[k] < USERS)
            def _(k=k):
                rs_merge(k, i - DELAY[k])
                if k < 4:
                    rs_send(k + 1, i - DELAY[k])

        return carry

    lax.fori_loop(USERS, 2 * USERS, student_slot, 0)

    own_all = oc[...].reshape(OWN_ALL, WIDTH)
    parts = []
    for u in range(USERS):
        _, keep, _ = rs_plan(4, u)
        parts.append(acc[u, keep])
    pooled = dot(jnp.concatenate(parts, axis=0), value_weight[...].astype(F32), 1, 0, HIGHEST)
    normed = pooled * lax.rsqrt(jnp.mean(pooled * pooled, axis=1, keepdims=True) + 1e-6)
    mixed = (normed * own_all).astype(BF16)
    t_hidden = gelu(dot(mixed, head_weight[...]))
    t_logit = SOFT_CAP * jnp.tanh(
        jnp.sum(t_hidden * head_vector[...], axis=1, keepdims=True) / SOFT_CAP
    )
    lane = lax.broadcasted_iota(jnp.int32, (OWN_ALL, 128), 1)
    sub = lax.broadcasted_iota(jnp.int32, (OWN_ALL, 128), 0)
    logits_out[...] = jnp.sum(
        jnp.where(lane == sub % OWN, jnp.broadcast_to(t_logit, (OWN_ALL, 128)), 0.0).reshape(
            USERS, OWN, 128
        ),
        axis=1,
    )

    inter = interest[...].reshape(OWN_ALL, WIDTH)
    hid = (
        dot(inter, pooling_weight[...], 1, 0, HIGHEST)
        + dot(own_all, itemwise_weight[...], 1, 0, HIGHEST)
        + hidden_bias[...]
    )
    th = jnp.tanh(GELU_K * (hid + GELU_C * hid * hid * hid))
    s_hidden = 0.5 * hid * (1.0 + th)
    slope = 0.5 * (1.0 + th) + 0.5 * hid * (1.0 - th * th) * (
        GELU_K * (1.0 + 3.0 * GELU_C * hid * hid)
    )
    s_tanh = jnp.tanh(
        jnp.sum(s_hidden * output_vector[...], axis=1, keepdims=True) / SOFT_CAP
    )
    s_logit = SOFT_CAP * s_tanh

    s_exp = jnp.broadcast_to(jnp.exp(s_logit), (OWN_ALL, 128))
    t_exp = jnp.broadcast_to(jnp.exp(t_logit), (OWN_ALL, 128))

    def exchange(slots, count, me, peer, send_sem, recv_sem):
        def copy(k, to):
            return pltpu.make_async_remote_copy(
                src_ref=slots.at[me],
                dst_ref=slots.at[me],
                send_sem=send_sem.at[k],
                recv_sem=recv_sem.at[me],
                device_id=to,
                device_id_type=MESH,
            )

        def arrival(k):
            return pltpu.make_async_remote_copy(
                src_ref=slots.at[me],
                dst_ref=slots.at[k],
                send_sem=send_sem.at[k],
                recv_sem=recv_sem.at[k],
                device_id=peer(k),
                device_id_type=MESH,
            )

        def start():
            for d in range(1, count):
                k = (me + d) % count
                copy(k, peer(k)).start()

        def wait():
            for d in range(1, count):
                k = (me + d) % count
                arrival(k).wait_recv()
            for d in range(1, count):
                k = (me + d) % count
                copy(k, peer(k)).wait_send()

        return start, wait

    rows_t[0] = jnp.transpose(inter)
    rows_t[1] = jnp.transpose(own_all)
    st1[place8, 0] = jnp.sum(s_exp.reshape(USERS, OWN, 128), axis=1)
    st1[place8, 1] = jnp.sum(t_exp.reshape(USERS, OWN, 128), axis=1)
    start, wait = exchange(st1, 8, place8, peer8, st1_s, st1_r)
    start()
    wait()
    st2[place16] = jnp.sum(st1[...], axis=0)
    start, wait = exchange(st2, 16, place16, peer16, st2_s, st2_r)
    start()
    wait()
    sums = jnp.sum(st2[...], axis=0)

    def wide(v):
        return jnp.broadcast_to(v[:, None, :], (USERS, OWN, 128)).reshape(OWN_ALL, 128)

    scale = math.sqrt(4 * CAND_DEV / USERS)
    logit_grad = scale * (s_exp / wide(sums[0]) - t_exp / wide(sums[1]))
    draw = logit_grad[:, :1] * (1.0 - s_tanh * s_tanh)
    dhid = draw * output_vector[...] * slope
    hidden_grad = jnp.sum(dhid, axis=0, keepdims=True)
    output_grad = jnp.sum(s_hidden * draw, axis=0, keepdims=True)
    dh[...] = dhid
    dinter = dot(dhid, pooling_weight[...], 1, 1, HIGHEST)
    for u in range(USERS):
        d = dot(dinter[u * OWN : u * OWN + OWN, :], short[u].astype(F32), 1, 1, HIGHEST)
        datt[u] = jnp.where(short_ok(u), d, 0.0)

    def mlp_half(h, carry):
        mlp[h] = dot(rows_t[h], dh[...], 1, 0, HIGHEST)
        return carry

    lax.fori_loop(0, 2, mlp_half, 0)

    def back_user(u, carry):
        msum[...] = jnp.zeros_like(msum)

        def group(cg, inner):
            total = msum[...]
            for j in range(CGROUP):
                c = cg * CGROUP + j
                m = jnp.where(pre[u, c] > 0.0, datt[u, pl.ds(c, 1), :], 0.0)
                total = total + m
                wb[0, j * 128 : j * 128 + 128, :] = m.astype(BF16)
            msum[...] = total
            g = dot(wb[0], short[u])
            add = pg[...]
            for j in range(CGROUP):
                c = cg * CGROUP + j
                add = add + g[j * 128 : j * 128 + 128, :] * oc[u, pl.ds(c, 1), :]
            pg[...] = add
            return inner

        lax.fori_loop(0, OWN // CGROUP, group, 0)
        mtot[...] += msum[...]
        eg[...] += dot(msum[...], short[u].astype(F32), 1, 0, HIGHEST)
        return carry

    lax.fori_loop(0, USERS, back_user, 0)

    g_row = diag_row(jnp.sum(mtot[...], axis=1, keepdims=True))
    sm1[place8] = jnp.concatenate(
        [
            jnp.concatenate([g_row, jnp.zeros_like(g_row)], axis=1),
            hidden_grad,
            output_grad,
            jnp.zeros((5, WIDTH), F32),
        ],
        axis=0,
    )
    small_start, small_wait = exchange(sm1, 8, place8, peer8, sm1_s, sm1_r)
    small_start()

    def put(first, value):
        for c in range(value.shape[0] // 8):
            at = first // 8 + c
            half, rest = divmod(at, 48)
            gb[half, rest // 3, (rest % 3) * 8 : (rest % 3) * 8 + 8, :] = value[c * 8 : c * 8 + 8, :]

    put(0, pg[...])
    put(128, eg[...])
    put(256, mlp[0])
    put(512, mlp[1])

    swap = pltpu.make_async_remote_copy(
        src_ref=gb.at[1 - core],
        dst_ref=r0,
        send_sem=a0_s,
        recv_sem=a0_r,
        device_id=sibling,
        device_id_type=MESH,
    )
    swap.start()
    small_wait()
    sm2[place16] = jnp.sum(sm1[...], axis=0)
    small_start, small_wait = exchange(sm2, 16, place16, peer16, sm2_s, sm2_r)
    small_start()
    swap.wait()
    r0[...] = r0[...] + gb[core]

    def scatter(k, slot):
        return pltpu.make_async_remote_copy(
            src_ref=r0.at[k],
            dst_ref=r1.at[slot],
            send_sem=a1_s.at[k],
            recv_sem=a1_r.at[slot],
            device_id=peer16(k),
            device_id_type=MESH,
        )

    others = [(place16 + d) % 16 for d in range(1, 16)]
    for k in others:
        scatter(k, place16).start()
    r1[place16] = r0[place16]
    for k in others:
        scatter(k, k).wait_recv()
    r2[y] = jnp.sum(r1[...], axis=0)
    start, wait = exchange(r2, 4, y, peer_y, a2_s, a2_r)
    start()
    wait()
    grads_out[core, place16] = jnp.sum(r2[...], axis=0)

    def spread(k, slot):
        return pltpu.make_async_remote_copy(
            src_ref=grads_out.at[core, slot],
            dst_ref=grads_out.at[core, slot],
            send_sem=a3_s.at[k],
            recv_sem=a3_r.at[slot],
            device_id=peer16(k),
            device_id_type=MESH,
        )

    for k in others:
        spread(k, place16).start()
    for k in others:
        scatter(k, place16).wait_send()
    small_wait()
    small_out[...] = jnp.sum(sm2[...], axis=0)
    for k in others:
        spread(k, k).wait_recv()
    last = pltpu.make_async_remote_copy(
        src_ref=grads_out.at[core],
        dst_ref=grads_out.at[core],
        send_sem=a4_s,
        recv_sem=a4_r,
        device_id=sibling,
        device_id_type=MESH,
    )
    last.start()
    for k in others:
        spread(k, place16).wait_send()
    last.wait_send()
    pltpu.make_async_remote_copy(
        src_ref=grads_out.at[core],
        dst_ref=grads_out.at[1 - core],
        send_sem=a4_s,
        recv_sem=a4_r,
        device_id=sibling,
        device_id_type=MESH,
    ).wait_recv()


def finish_kernel(
    logits,
    grads,
    small,
    pair_weight,
    event_weight,
    scoring_bias,
    weigher,
    logits_out,
    pair_out,
    event_out,
    scoring_out,
    weigher_out,
    pooling_out,
    itemwise_out,
    hidden_out,
    output_out,
):
    flat = grads[...].reshape(768, WIDTH)
    w = weigher[...]
    pair = jnp.transpose(flat[:128])
    event = jnp.transpose(flat[128:256])
    g = small[0:1, :128]
    pair_out[...] = pair * w
    event_out[...] = event * w
    scoring_out[...] = g * w
    weigher_out[...] = scoring_bias[...] * g + jnp.sum(
        pair * pair_weight[...] + event * event_weight[...], axis=0, keepdims=True
    )
    pooling_out[...] = flat[256:512]
    itemwise_out[...] = flat[512:768]
    hidden_out[...] = small[1:2, :]
    output_out[...] = small[2:3, :]
    logits_out[...] = logits[:, :OWN]


def body(
    history,
    candidates,
    short_hist,
    lengths,
    pad_mask,
    short_mask,
    query_gain,
    value_weight,
    head_weight,
    head_vector,
    pair_weight,
    event_weight,
    scoring_bias,
    weigher,
    pooling_weight,
    itemwise_weight,
    hidden_bias,
    output_vector,
):
    vmem = pl.BlockSpec(memory_space=pltpu.VMEM)
    row = lambda v: v.reshape(1, -1)
    dma = pltpu.SemaphoreType.DMA
    logits, grads, small = pl.pallas_call(
        main_kernel,
        out_shape=(
            jax.ShapeDtypeStruct((USERS, 128), F32),
            jax.ShapeDtypeStruct((2, 16, 24, WIDTH), F32),
            jax.ShapeDtypeStruct((8, WIDTH), F32),
        ),
        in_specs=[
            pl.BlockSpec(memory_space=pltpu.SMEM),
            pl.BlockSpec(memory_space=pl.ANY),
        ]
        + [vmem] * 16,
        out_specs=(vmem, vmem, vmem),
        scratch_shapes=[
            pltpu.VMEM((USERS, EVENTS, WIDTH), BF16),
            pltpu.VMEM((CAND_DEV, WIDTH), BF16),
            pltpu.VMEM((CAND_DEV, EVENTS), F32),
            pltpu.VMEM((CAND_DEV, EVENTS), BF16),
            pltpu.VMEM((CAND_DEV, 128), F32),
            pltpu.VMEM((CAND_DEV, 128), F32),
            pltpu.VMEM((USERS, BLOCKS, OWN, WIDTH), F32),
            pltpu.VMEM((5, USERS, 4, 8, 128), F32),
            pltpu.VMEM((USERS, 16, OWN, WIDTH), F32),
            pltpu.VMEM((USERS, 8, OWN, WIDTH), F32),
            pltpu.VMEM((USERS, 4, OWN, WIDTH), F32),
            pltpu.VMEM((USERS, 2, OWN, WIDTH), F32),
            pltpu.VMEM((USERS, 1, OWN, WIDTH), F32),
            pltpu.VMEM((USERS, 6, 8, 128), F32),
            pltpu.VMEM((USERS, OWN, WIDTH), F32),
            pltpu.VMEM((SCORE_H, WIDTH), F32),
            pltpu.VMEM((SCORE_H, WIDTH), F32),
            pltpu.VMEM((SCORE_H, WIDTH), F32),
            pltpu.VMEM((SCORE_H, WIDTH), F32),
            pltpu.VMEM((2, CGROUP * SCORE_H, WIDTH), BF16),
            pltpu.VMEM((USERS, OWN, SCORE_H, SHORT), F32),
            pltpu.VMEM((USERS, OWN, SHORT), F32),
            pltpu.VMEM((USERS, OWN, WIDTH), F32),
            pltpu.VMEM((USERS, OWN, SHORT), F32),
            pltpu.VMEM((SCORE_H, WIDTH), F32),
            pltpu.VMEM((SCORE_H, SHORT), F32),
            pltpu.VMEM((SCORE_H, SHORT), F32),
            pltpu.VMEM((SCORE_H, WIDTH), F32),
            pltpu.VMEM((2, WIDTH, OWN_ALL), F32),
            pltpu.VMEM((OWN_ALL, WIDTH), F32),
            pltpu.VMEM((2, WIDTH, WIDTH), F32),
            pltpu.VMEM((8, 2, USERS, 128), F32),
            pltpu.VMEM((16, 2, USERS, 128), F32),
            pltpu.VMEM((8, 8, WIDTH), F32),
            pltpu.VMEM((16, 8, WIDTH), F32),
            pltpu.VMEM((2, 16, 24, WIDTH), F32),
            pltpu.VMEM((16, 24, WIDTH), F32),
            pltpu.VMEM((16, 24, WIDTH), F32),
            pltpu.VMEM((4, 24, WIDTH), F32),
            dma((USERS,)),
            dma((5, USERS)),
            dma((5, USERS)),
            dma((5, USERS)),
            dma((5, USERS)),
            dma((8,)),
            dma((8,)),
            dma((16,)),
            dma((16,)),
            dma((8,)),
            dma((8,)),
            dma((16,)),
            dma((16,)),
            dma,
            dma,
            dma((16,)),
            dma((16,)),
            dma((4,)),
            dma((4,)),
            dma((16,)),
            dma((16,)),
            dma,
            dma,
        ],
        compiler_params=pltpu.CompilerParams(
            collective_id=0, has_side_effects=True, vmem_limit_bytes=62 * 1024 * 1024
        ),
        name="main_kernel",
    )(
        lengths,
        history,
        candidates,
        short_hist,
        pad_mask,
        short_mask,
        row(query_gain),
        value_weight,
        head_weight,
        row(head_vector),
        pair_weight,
        event_weight,
        row(scoring_bias),
        row(weigher),
        pooling_weight,
        itemwise_weight,
        row(hidden_bias),
        row(output_vector),
    )
    out = pl.pallas_call(
        finish_kernel,
        out_shape=(
            jax.ShapeDtypeStruct((USERS, OWN), F32),
            jax.ShapeDtypeStruct((WIDTH, SCORE_H), F32),
            jax.ShapeDtypeStruct((WIDTH, SCORE_H), F32),
            jax.ShapeDtypeStruct((1, SCORE_H), F32),
            jax.ShapeDtypeStruct((1, SCORE_H), F32),
            jax.ShapeDtypeStruct((WIDTH, WIDTH), F32),
            jax.ShapeDtypeStruct((WIDTH, WIDTH), F32),
            jax.ShapeDtypeStruct((1, WIDTH), F32),
            jax.ShapeDtypeStruct((1, WIDTH), F32),
        ),
        in_specs=[vmem] * 7,
        out_specs=(vmem,) * 9,
        name="finish_kernel",
    )(logits, grads, small, pair_weight, event_weight, row(scoring_bias), row(weigher))
    flat = lambda v: v.reshape(-1)
    return (
        out[0],
        out[1],
        out[2],
        flat(out[3]),
        flat(out[4]),
        out[5],
        out[6],
        flat(out[7]),
        flat(out[8]),
    )


def solution(mesh):
    placed = (P(None, "ctx", None), P(None, "cand", None), P(), P(), P(None, "ctx")) + (P(),) * 13
    return jax.shard_map(
        body,
        mesh=mesh,
        in_specs=placed,
        out_specs=(P(None, ("cand", "ctx")),) + (P(),) * 8,
        check_vma=False,
    )
```

```python
import functools
import math

import jax
import jax.numpy as jnp
from jax import lax
from jax.experimental import pallas as pl
from jax.experimental.pallas import tpu as pltpu
from jax.sharding import PartitionSpec as P

NEG_FILL = -1e30
NEG_CLAMP = -1e29
SOFT_CAP = 10.0
HIGHEST = lax.Precision.HIGHEST
F32 = jnp.float32
BF16 = jnp.bfloat16
MESH = pl.DeviceIdType.MESH

USERS = 8
CAND_DEV = 512
EVENTS = 2048
WIDTH = 256
SHORT = 256
SCORE_H = 128
OWN = 16
BLOCKS = 32
OWN_ALL = USERS * OWN
CGROUP = 4
DELAY = (3, 5, 7, 9, 11)
SLOTS = USERS + DELAY[4]
GELU_K = math.sqrt(2.0 / math.pi)
GELU_C = 0.044715


def dot(a, b, ca=1, cb=0, precision=None):
    return lax.dot_general(
        a, b, (((ca,), (cb,)), ((), ())), precision=precision, preferred_element_type=F32
    )


def gelu(p):
    return 0.5 * p * (1.0 + jnp.tanh(GELU_K * (p + GELU_C * p * p * p)))


def diag_row(col, n=128):
    lane = lax.broadcasted_iota(jnp.int32, (n, n), 1)
    sub = lax.broadcasted_iota(jnp.int32, (n, n), 0)
    return jnp.sum(jnp.where(lane == sub, jnp.broadcast_to(col, (n, n)), 0.0), axis=0, keepdims=True)


def to_column(row):
    return jnp.transpose(jnp.broadcast_to(row, (128, 128)))


def main_kernel(
    lengths,
    history,
    candidates_hbm,
    short_hbm,
    value_hbm,
    head_hbm,
    pair_hbm,
    event_hbm,
    pooling_hbm,
    itemwise_hbm,
    pad_mask,
    short_mask,
    query_gain,
    head_vector,
    scoring_bias,
    weigher,
    hidden_bias,
    output_vector,
    logits_out,
    mlp_out,
    att_out,
    small_out,
    hist,
    candidates,
    short,
    value_weight,
    head_weight,
    pair_weight,
    event_weight,
    pooling_weight,
    itemwise_weight,
    qs,
    scores,
    probs,
    inv_col,
    lse_col,
    top_part,
    top_col,
    sum_part,
    acc,
    lse,
    rv0,
    rv1,
    rv2,
    rv3,
    rv4,
    rl,
    oc,
    pw_t,
    ew_t,
    w_full,
    b_full,
    wb,
    pre,
    att,
    interest,
    datt,
    exps,
    unit_sums,
    row_scale,
    cand_scale,
    rows_t,
    dh,
    mlp,
    st1,
    st2,
    sm1,
    sm2,
    gb0,
    gb1,
    r00,
    r01,
    r10,
    r11,
    r20,
    r21,
    hist_sem,
    cand_sem,
    load_sem,
    rs_vs,
    rs_vr,
    rs_ls,
    rs_lr,
    st1_s,
    st1_r,
    st2_s,
    st2_r,
    sm1_s,
    sm1_r,
    sm2_s,
    sm2_r,
    a0_s,
    a0_r,
    a1_s,
    a1_r,
    a2_s,
    a2_r,
    a3_s,
    a3_r,
    a4_s,
    a4_r,
):
    loads = (
        (short_hbm, short),
        (pair_hbm, pair_weight),
        (event_hbm, event_weight),
        (pooling_hbm, pooling_weight),
        (itemwise_hbm, itemwise_weight),
        (value_hbm, value_weight),
        (head_hbm, head_weight),
    )
    rv = (rv0, rv1, rv2, rv3, rv4)
    cand = lax.axis_index("cand")
    ctx = lax.axis_index("ctx")
    x = ctx % 4
    y_hi = (ctx // 4) % 2
    z = ctx // 8
    y_lo = cand // 2
    core = cand % 2
    y = y_hi * 2 + y_lo
    place8 = y_hi * 4 + cand
    place16 = z * 4 + x

    def peer8(k):
        return (k % 4, z * 8 + (k // 4) * 4 + x)

    def peer16(k):
        return (cand, (k // 4) * 8 + y_hi * 4 + k % 4)

    def peer_y(k):
        return ((k % 2) * 2 + core, z * 8 + (k // 2) * 4 + x)

    sibling = (y_lo * 2 + 1 - core, ctx)

    def hist_copy(u):
        return pltpu.make_async_copy(history.at[u], hist.at[u], hist_sem.at[u])

    def cand_copy(u):
        return pltpu.make_async_copy(candidates_hbm.at[u], candidates.at[u], cand_sem.at[u])

    def load(k):
        return pltpu.make_async_copy(loads[k][0], loads[k][1], load_sem.at[k])

    barrier = pltpu.get_barrier_semaphore()
    for d in range(1, 8):
        pl.semaphore_signal(barrier, inc=1, device_id=peer8((place8 + d) % 8), device_id_type=MESH)
    for d in range(1, 16):
        pl.semaphore_signal(
            barrier, inc=1, device_id=peer16((place16 + d) % 16), device_id_type=MESH
        )
    for u in range(USERS):
        cand_copy(u).start()
        hist_copy(u).start()
    for k in range(len(loads)):
        load(k).start()

    def set_up():
        for k in range(len(loads)):
            load(k).wait()
        pw_t[...] = jnp.transpose(pair_weight[...])
        ew_t[...] = jnp.transpose(event_weight[...])
        wc = to_column(weigher[...])
        bc = to_column(scoring_bias[...])
        w_full[:, :128] = wc
        w_full[:, 128:] = wc
        b_full[:, :128] = bc
        b_full[:, 128:] = bc
        for u in range(USERS):
            oc[u] = candidates[u, pl.ds(pl.multiple_of(ctx * OWN, OWN), OWN), :].astype(F32)
        unit_sums[...] = jnp.zeros_like(unit_sums)

    stride1 = 1 + 7 * core
    stride2 = 8 - 7 * core
    c1 = (ctx // stride1) % 4
    c2 = (ctx // stride2) % 4

    def bits_of(c):
        low, high = c % 2, c // 2
        return low + high - 2 * low * high, high

    def rs_plan(k, u):
        q = u % 2
        a1, b1 = bits_of(c1)
        a2, b2 = bits_of(c2)
        bits = (a1 + q * (b1 - a1), b1 + q * (a1 - b1), a2 + q * (b2 - a2), b2 + q * (a2 - b2), y_hi)
        start = 0
        for j in range(k):
            start = start + bits[j] * (16 >> j)
        n = 16 >> k
        keep = start + bits[k] * n
        send = start + (1 - bits[k]) * n
        if k == 4:
            partner = ctx + (1 - 2 * y_hi) * 4
        else:
            c, stride = (c1, stride1) if k < 2 else (c2, stride2)
            pa = c + 1 - 2 * (c % 2)
            pb = 3 - c
            pc = pa + q * (pb - pa) if k % 2 == 0 else pb + q * (pa - pb)
            partner = ctx + (pc - c) * stride
        return (cand, partner), keep, send

    def rs_copies(k, u):
        device, _, send = rs_plan(k, u)
        n = 16 >> k
        value = pltpu.make_async_remote_copy(
            src_ref=acc.at[u, pl.ds(send, n)],
            dst_ref=rv[k].at[u],
            send_sem=rs_vs.at[k, u],
            recv_sem=rs_vr.at[k, u],
            device_id=device,
            device_id_type=MESH,
        )
        if k == 0:
            src, dst = lse.at[k, u, pl.ds(send // 8, 2)], rl.at[u, pl.ds(0, 2)]
        else:
            src, dst = lse.at[k, u, pl.ds(send // 8, 1)], rl.at[u, pl.ds(1 + k, 1)]
        weight = pltpu.make_async_remote_copy(
            src_ref=src,
            dst_ref=dst,
            send_sem=rs_ls.at[k, u],
            recv_sem=rs_lr.at[k, u],
            device_id=device,
            device_id_type=MESH,
        )
        return value, weight

    def rs_send(k, u):
        for copy in rs_copies(k, u):
            copy.start()

    def rs_merge(k, u):
        for copy in rs_copies(k, u):
            copy.wait()
        _, keep, _ = rs_plan(k, u)
        n = 16 >> k
        rows = 2 if k == 0 else 1
        per_row = min(n, 8)
        for r in range(rows):
            row = keep // 8 + r
            mine = lse[k, u, row]
            other = rl[u, (r if k == 0 else 1 + k)]
            top = jnp.maximum(mine, other)
            e_mine = jnp.exp(mine - top)
            e_other = jnp.exp(other - top)
            total = e_mine + e_other
            share = e_other / total
            if k < 4:
                lse[k + 1, u, row] = top + jnp.log(total)
            share16 = jnp.concatenate([share, share], axis=0)
            lane = lax.broadcasted_iota(jnp.int32, (16, 128), 1)
            sub = lax.broadcasted_iota(jnp.int32, (16, 128), 0)
            for b in range(per_row):
                at = keep + r * 8 + b
                off = (at % 8) * 16
                col = jnp.sum(
                    jnp.where(lane - sub == off, share16, 0.0), axis=1, keepdims=True
                )
                own = acc[u, at]
                got = rv[k][u, r * 8 + b]
                acc[u, at] = own + col * (got - own)

    def teacher_user(u):
        q = u % 2
        gain = query_gain[...] * (1.0 / 16.0)
        cand_copy(u).wait()
        for pos in range(BLOCKS):
            p4, p3, p2, p1, p0 = ((pos >> s) & 1 for s in (4, 3, 2, 1, 0))
            first = 2 * (p3 + q * (p4 - p3)) + (p4 ^ p3)
            second = 2 * (p1 + q * (p2 - p1)) + (p2 ^ p1)
            block = first * stride1 + second * stride2 + p0 * 4
            rows = candidates[u, pl.ds(pl.multiple_of(block * 16, 16), 16), :]
            qs[pos * 16 : pos * 16 + 16, :] = (rows.astype(F32) * gain).astype(BF16)
        spot = lax.broadcasted_iota(jnp.int32, (1, EVENTS), 1) + ctx * EVENTS
        ok = (spot < lengths[u]) & ((pad_mask[pl.ds(u, 1), :] == 1) | (spot == 0))
        bias = jnp.where(ok, 0.0, NEG_FILL)
        hist_copy(u).wait()
        for t in range(4):
            cols = slice(t * 512, t * 512 + 512)
            s = dot(qs[...], hist[u, cols, :], 1, 1) + bias[:, cols]
            scores[:, cols] = s
            top = s[:, :128]
            for g in range(1, 4):
                top = jnp.maximum(top, s[:, g * 128 : g * 128 + 128])
            top_part[...] = top if t == 0 else jnp.maximum(top_part[...], top)
        top = jnp.maximum(jnp.max(top_part[...], axis=1, keepdims=True), NEG_CLAMP)
        top_col[...] = jnp.broadcast_to(top, (CAND_DEV, 128))
        for r in range(16):
            rows = slice(r * 32, r * 32 + 32)
            m = top_col[rows, :]
            total = None
            for g in range(16):
                cols = slice(g * 128, g * 128 + 128)
                e = jnp.exp(scores[rows, cols] - m)
                probs[rows, cols] = e.astype(BF16)
                total = e if total is None else total + e
            sum_part[rows, :] = total
        total = jnp.sum(sum_part[...], axis=1, keepdims=True)
        some = total > 0.0
        safe = jnp.where(some, total, 1.0)
        lse_col[...] = jnp.where(some, top_col[...] + jnp.log(safe), NEG_FILL)
        inv_col[...] = jnp.broadcast_to(1.0 / safe, (CAND_DEV, 128))
        lane = lax.broadcasted_iota(jnp.int32, (128, 128), 1)
        sub = lax.broadcasted_iota(jnp.int32, (128, 128), 0)
        for g in range(4):
            rows = slice(g * 128, g * 128 + 128)
            row = jnp.sum(jnp.where(lane == sub, lse_col[rows, :], 0.0), axis=0, keepdims=True)
            lse[0, u, g] = jnp.broadcast_to(row, (8, 128))
        for t in range(2):
            rows = slice(t * 256, t * 256 + 256)
            out = dot(probs[rows, :], hist[u])
            inv = inv_col[rows, :]
            acc[u, t * 16 : t * 16 + 16, :, :128] = (out[:, :128] * inv).reshape(16, 16, 128)
            acc[u, t * 16 : t * 16 + 16, :, 128:] = (out[:, 128:] * inv).reshape(16, 16, 128)

    def short_ok(u):
        spot = lax.broadcasted_iota(jnp.int32, (1, SHORT), 1)
        return (short_mask[pl.ds(u, 1), :] == 1) | (spot == 0)

    def student_user(u):
        for cg in range(OWN // CGROUP):
            for j in range(CGROUP):
                c = cg * CGROUP + j
                w = pw_t[...] * oc[u, pl.ds(c, 1), :] + ew_t[...]
                high = w.astype(BF16)
                wb[cg, 0, j * 128 : j * 128 + 128, :] = high
                wb[cg, 1, j * 128 : j * 128 + 128, :] = (w - high.astype(F32)).astype(BF16)
            p = dot(wb[cg, 0], short[u], 1, 1) + dot(wb[cg, 1], short[u], 1, 1)
            for j in range(CGROUP):
                c = cg * CGROUP + j
                pj = p[j * 128 : j * 128 + 128, :] + b_full[...]
                pre[u, c] = pj
                att[u, pl.ds(c, 1), :] = jnp.sum(
                    jnp.maximum(pj, 0.0) * w_full[...], axis=0, keepdims=True
                )
        weights = jnp.where(short_ok(u), att[u], 0.0)
        interest[u] = dot(weights, short[u].astype(F32), 1, 0, HIGHEST)

    def back_user(u):
        for cg in range(OWN // CGROUP):
            cols = []
            for j in range(CGROUP):
                c = cg * CGROUP + j
                m = jnp.where(pre[u, c] > 0.0, datt[u, pl.ds(c, 1), :], 0.0)
                wb[cg, 0, j * 128 : j * 128 + 128, :] = m.astype(BF16)
                cols.append(jnp.sum(m, axis=1, keepdims=True))
            g = dot(wb[cg, 0], short[u])
            for j in range(CGROUP):
                pre[u, cg * CGROUP + j] = g[j * 128 : j * 128 + 128, :]
            lane = lax.broadcasted_iota(jnp.int32, (SCORE_H, OWN_ALL), 1)
            units = unit_sums[...]
            for j in range(CGROUP):
                units = jnp.where(lane == u * OWN + cg * CGROUP + j, cols[j], units)
            unit_sums[...] = units

    def reduce_steps(i):
        for k in reversed(range(5)):
            u = i - DELAY[k]

            def step(k=k, u=u):
                rs_merge(k, u)
                if k < 4:
                    rs_send(k + 1, u)

            pl.when((u >= 0) & (u < USERS))(step)

    def teacher_slot(i, carry):
        teacher_user(i)

        @pl.when(i == 0)
        def _():
            pl.semaphore_wait(barrier, 22)

        rs_send(0, i)
        reduce_steps(i)
        return carry

    lax.fori_loop(0, USERS, teacher_slot, 0)
    set_up()

    def student_slot(i, carry):
        student_user(i - USERS)
        reduce_steps(i)
        return carry

    lax.fori_loop(USERS, 2 * USERS, student_slot, 0)

    own_all = oc[...].reshape(OWN_ALL, WIDTH)
    inter = interest[...].reshape(OWN_ALL, WIDTH)
    hid = (
        dot(inter, pooling_weight[...], 1, 0, HIGHEST)
        + dot(own_all, itemwise_weight[...], 1, 0, HIGHEST)
        + hidden_bias[...]
    )
    th = jnp.tanh(GELU_K * (hid + GELU_C * hid * hid * hid))
    s_hidden = 0.5 * hid * (1.0 + th)
    slope = 0.5 * (1.0 + th) + 0.5 * hid * (1.0 - th * th) * (
        GELU_K * (1.0 + 3.0 * GELU_C * hid * hid)
    )
    s_tanh = jnp.tanh(jnp.sum(s_hidden * output_vector[...], axis=1, keepdims=True) / SOFT_CAP)
    draw = 1.0 - s_tanh * s_tanh
    dhid = draw * output_vector[...] * slope
    dinter = dot(dhid, pooling_weight[...], 1, 1, HIGHEST)
    for u in range(USERS):
        d = dot(dinter[u * OWN : u * OWN + OWN, :], short[u].astype(F32), 1, 1, HIGHEST)
        datt[u] = jnp.where(short_ok(u), d, 0.0)
    dh[0] = dhid
    dh[1] = s_hidden * draw
    s_exp = jnp.broadcast_to(jnp.exp(SOFT_CAP * s_tanh), (OWN_ALL, 128))
    exps[0] = s_exp
    rows_t[0] = jnp.transpose(inter)
    rows_t[1] = jnp.transpose(own_all)

    def back_slot(i, carry):
        back_user(i - 2 * USERS)
        reduce_steps(i)
        return carry

    lax.fori_loop(2 * USERS, SLOTS, back_slot, 0)

    own_all = oc[...].reshape(OWN_ALL, WIDTH)
    parts = []
    for u in range(USERS):
        _, keep, _ = rs_plan(4, u)
        parts.append(acc[u, keep])
    pooled = dot(jnp.concatenate(parts, axis=0), value_weight[...].astype(F32), 1, 0, HIGHEST)
    normed = pooled * lax.rsqrt(jnp.mean(pooled * pooled, axis=1, keepdims=True) + 1e-6)
    mixed = (normed * own_all).astype(BF16)
    t_hidden = gelu(dot(mixed, head_weight[...]))
    t_logit = SOFT_CAP * jnp.tanh(
        jnp.sum(t_hidden * head_vector[...], axis=1, keepdims=True) / SOFT_CAP
    )
    lane = lax.broadcasted_iota(jnp.int32, (OWN_ALL, 128), 1)
    sub = lax.broadcasted_iota(jnp.int32, (OWN_ALL, 128), 0)
    logits_out[...] = jnp.sum(
        jnp.where(lane == sub % OWN, jnp.broadcast_to(t_logit, (OWN_ALL, 128)), 0.0).reshape(
            USERS, OWN, 128
        ),
        axis=1,
    )

    t_exp = jnp.broadcast_to(jnp.exp(t_logit), (OWN_ALL, 128))
    exps[1] = t_exp

    def exchange(slots, count, me, peer, send_sem, recv_sem):
        def copy(k, to):
            return pltpu.make_async_remote_copy(
                src_ref=slots.at[me],
                dst_ref=slots.at[me],
                send_sem=send_sem.at[k],
                recv_sem=recv_sem.at[me],
                device_id=to,
                device_id_type=MESH,
            )

        def arrival(k):
            return pltpu.make_async_remote_copy(
                src_ref=slots.at[me],
                dst_ref=slots.at[k],
                send_sem=send_sem.at[k],
                recv_sem=recv_sem.at[k],
                device_id=peer(k),
                device_id_type=MESH,
            )

        def start():
            for d in range(1, count):
                k = (me + d) % count
                copy(k, peer(k)).start()

        def wait():
            for d in range(1, count):
                k = (me + d) % count
                arrival(k).wait_recv()
            for d in range(1, count):
                k = (me + d) % count
                copy(k, peer(k)).wait_send()

        return start, wait

    st1[place8, 0] = jnp.sum(exps[0].reshape(USERS, OWN, 128), axis=1)
    st1[place8, 1] = jnp.sum(t_exp.reshape(USERS, OWN, 128), axis=1)

    def more_back(first, last):
        def one(u, carry):
            back_user(u)
            return carry

        lax.fori_loop(first, last, one, 0)

    done = SLOTS - 2 * USERS
    start, wait = exchange(st1, 8, place8, peer8, st1_s, st1_r)
    start()
    more_back(done, done + 3)
    wait()
    st2[place16] = jnp.sum(st1[...], axis=0)
    start, wait = exchange(st2, 16, place16, peer16, st2_s, st2_r)
    start()
    more_back(done + 3, USERS)
    wait()
    sums = jnp.sum(st2[...], axis=0)

    def wide(v):
        return jnp.broadcast_to(v[:, None, :], (USERS, OWN, 128)).reshape(OWN_ALL, 128)

    scale = math.sqrt(4 * CAND_DEV / USERS)
    logit_grad = scale * (exps[0] / wide(sums[0]) - exps[1] / wide(sums[1]))
    row_scale[:, :128] = logit_grad
    row_scale[:, 128:] = logit_grad
    cand_scale[...] = row_scale[...] * oc[...].reshape(OWN_ALL, WIDTH)
    dh[0] = dh[0] * row_scale[...]
    dh[1] = dh[1] * row_scale[...]

    def mlp_half(h, carry):
        mlp[h] = dot(rows_t[h], dh[0], 1, 0, HIGHEST)
        return carry

    lax.fori_loop(0, 2, mlp_half, 0)

    others = [(place16 + d) % 16 for d in range(1, 16)]

    def all_reduce(n, gb, r0, r1, r2, out):
        def swap():
            return pltpu.make_async_remote_copy(
                src_ref=gb.at[1 - core],
                dst_ref=r0,
                send_sem=a0_s.at[n],
                recv_sem=a0_r.at[n],
                device_id=sibling,
                device_id_type=MESH,
            )

        def scatter(k, slot):
            return pltpu.make_async_remote_copy(
                src_ref=r0.at[k],
                dst_ref=r1.at[slot],
                send_sem=a1_s.at[n, k],
                recv_sem=a1_r.at[n, slot],
                device_id=peer16(k),
                device_id_type=MESH,
            )

        def spread(k, slot):
            return pltpu.make_async_remote_copy(
                src_ref=out.at[core, slot],
                dst_ref=out.at[core, slot],
                send_sem=a3_s.at[n, k],
                recv_sem=a3_r.at[n, slot],
                device_id=peer16(k),
                device_id_type=MESH,
            )

        def last(slot):
            return pltpu.make_async_remote_copy(
                src_ref=out.at[core],
                dst_ref=out.at[slot],
                send_sem=a4_s.at[n],
                recv_sem=a4_r.at[n],
                device_id=sibling,
                device_id_type=MESH,
            )

        start_y, wait_y = exchange(r2, 4, y, peer_y, a2_s.at[n], a2_r.at[n])

        def step0():
            swap().start()

        def step1():
            swap().wait()
            r0[...] = r0[...] + gb[core]
            for k in others:
                scatter(k, place16).start()
            r1[place16] = r0[place16]

        def step2():
            for k in others:
                scatter(k, k).wait_recv()
            r2[y] = jnp.sum(r1[...], axis=0)
            start_y()

        def step3():
            wait_y()
            out[core, place16] = jnp.sum(r2[...], axis=0)
            for k in others:
                spread(k, place16).start()

        def step4():
            for k in others:
                spread(k, k).wait_recv()
            last(core).start()

        def step5():
            for k in others:
                scatter(k, place16).wait_send()
                spread(k, place16).wait_send()
            last(core).wait_send()
            last(1 - core).wait_recv()

        return step0, step1, step2, step3, step4, step5

    first = all_reduce(0, gb0, r00, r10, r20, mlp_out)
    second = all_reduce(1, gb1, r01, r11, r21, att_out)
    for h in range(2):
        gb0[h] = mlp[h].reshape(16, 16, WIDTH)
    first[0]()

    for ab in range(4):
        rows = slice(ab * 32, ab * 32 + 32)

        def add(i, carry):
            p, e = carry
            for j in range(OWN):
                g = pre[i, j, rows, :]
                p = p + g * cand_scale[pl.ds(i * OWN + j, 1), :]
                e = e + g * row_scale[pl.ds(i * OWN + j, 1), :]
            return p, e

        zero = jnp.zeros((32, WIDTH), F32)
        p, e = lax.fori_loop(0, USERS, add, (zero, zero))
        gb1[0, ab * 4 : ab * 4 + 4] = p.reshape(4, 8, WIDTH)
        gb1[1, ab * 4 : ab * 4 + 4] = e.reshape(4, 8, WIDTH)
        if ab == 1:
            first[1]()
    second[0]()
    lane = lax.broadcasted_iota(jnp.int32, (OWN_ALL, 128), 1)
    sub = lax.broadcasted_iota(jnp.int32, (OWN_ALL, 128), 0)
    scale_row = diag_row(row_scale[:, :128])
    g_row = diag_row(jnp.sum(unit_sums[...] * scale_row, axis=1, keepdims=True))
    sm1[place8] = jnp.concatenate(
        [
            jnp.concatenate([g_row, jnp.zeros_like(g_row)], axis=1),
            jnp.sum(dh[0], axis=0, keepdims=True),
            jnp.sum(dh[1], axis=0, keepdims=True),
            jnp.zeros((5, WIDTH), F32),
        ],
        axis=0,
    )
    start, wait = exchange(sm1, 8, place8, peer8, sm1_s, sm1_r)
    start()
    second[1]()
    first[2]()
    wait()
    sm2[place16] = jnp.sum(sm1[...], axis=0)
    start, wait = exchange(sm2, 16, place16, peer16, sm2_s, sm2_r)
    start()
    second[2]()
    first[3]()
    second[3]()
    wait()
    small_out[...] = jnp.sum(sm2[...], axis=0)
    first[4]()
    second[4]()
    first[5]()
    second[5]()


def finish_kernel(
    logits,
    mlp,
    att,
    small,
    pair_weight,
    event_weight,
    scoring_bias,
    weigher,
    logits_out,
    pair_out,
    event_out,
    scoring_out,
    weigher_out,
    pooling_out,
    itemwise_out,
    hidden_out,
    output_out,
):
    flat = mlp[...].reshape(512, WIDTH)
    attention = att[...].reshape(256, WIDTH)
    w = weigher[...]
    pair = jnp.transpose(attention[:128])
    event = jnp.transpose(attention[128:])
    g = small[0:1, :128]
    pair_out[...] = pair * w
    event_out[...] = event * w
    scoring_out[...] = g * w
    weigher_out[...] = scoring_bias[...] * g + jnp.sum(
        pair * pair_weight[...] + event * event_weight[...], axis=0, keepdims=True
    )
    pooling_out[...] = flat[:256]
    itemwise_out[...] = flat[256:]
    hidden_out[...] = small[1:2, :]
    output_out[...] = small[2:3, :]
    logits_out[...] = logits[:, :OWN]


def body(
    history,
    candidates,
    short_hist,
    lengths,
    pad_mask,
    short_mask,
    query_gain,
    value_weight,
    head_weight,
    head_vector,
    pair_weight,
    event_weight,
    scoring_bias,
    weigher,
    pooling_weight,
    itemwise_weight,
    hidden_bias,
    output_vector,
):
    vmem = pl.BlockSpec(memory_space=pltpu.VMEM)
    row = lambda v: v.reshape(1, -1)
    dma = pltpu.SemaphoreType.DMA
    logits, mlp, att, small = pl.pallas_call(
        main_kernel,
        out_shape=(
            jax.ShapeDtypeStruct((USERS, 128), F32),
            jax.ShapeDtypeStruct((2, 16, 16, WIDTH), F32),
            jax.ShapeDtypeStruct((2, 16, 8, WIDTH), F32),
            jax.ShapeDtypeStruct((8, WIDTH), F32),
        ),
        in_specs=[
            pl.BlockSpec(memory_space=pltpu.SMEM),
        ]
        + [pl.BlockSpec(memory_space=pl.ANY)] * 9
        + [vmem] * 8,
        out_specs=(vmem,) * 4,
        scratch_shapes=[
            pltpu.VMEM((USERS, EVENTS, WIDTH), BF16),
            pltpu.VMEM((USERS, CAND_DEV, WIDTH), BF16),
            pltpu.VMEM((USERS, SHORT, WIDTH), BF16),
            pltpu.VMEM((WIDTH, WIDTH), BF16),
            pltpu.VMEM((WIDTH, WIDTH), BF16),
            pltpu.VMEM((WIDTH, SCORE_H), F32),
            pltpu.VMEM((WIDTH, SCORE_H), F32),
            pltpu.VMEM((WIDTH, WIDTH), F32),
            pltpu.VMEM((WIDTH, WIDTH), F32),
            pltpu.VMEM((CAND_DEV, WIDTH), BF16),
            pltpu.VMEM((CAND_DEV, EVENTS), F32),
            pltpu.VMEM((CAND_DEV, EVENTS), BF16),
            pltpu.VMEM((CAND_DEV, 128), F32),
            pltpu.VMEM((CAND_DEV, 128), F32),
            pltpu.VMEM((CAND_DEV, 128), F32),
            pltpu.VMEM((CAND_DEV, 128), F32),
            pltpu.VMEM((CAND_DEV, 128), F32),
            pltpu.VMEM((USERS, BLOCKS, OWN, WIDTH), F32),
            pltpu.VMEM((5, USERS, 4, 8, 128), F32),
            pltpu.VMEM((USERS, 16, OWN, WIDTH), F32),
            pltpu.VMEM((USERS, 8, OWN, WIDTH), F32),
            pltpu.VMEM((USERS, 4, OWN, WIDTH), F32),
            pltpu.VMEM((USERS, 2, OWN, WIDTH), F32),
            pltpu.VMEM((USERS, 1, OWN, WIDTH), F32),
            pltpu.VMEM((USERS, 6, 8, 128), F32),
            pltpu.VMEM((USERS, OWN, WIDTH), F32),
            pltpu.VMEM((SCORE_H, WIDTH), F32),
            pltpu.VMEM((SCORE_H, WIDTH), F32),
            pltpu.VMEM((SCORE_H, WIDTH), F32),
            pltpu.VMEM((SCORE_H, WIDTH), F32),
            pltpu.VMEM((OWN // CGROUP, 2, CGROUP * SCORE_H, WIDTH), BF16),
            pltpu.VMEM((USERS, OWN, SCORE_H, SHORT), F32),
            pltpu.VMEM((USERS, OWN, SHORT), F32),
            pltpu.VMEM((USERS, OWN, WIDTH), F32),
            pltpu.VMEM((USERS, OWN, SHORT), F32),
            pltpu.VMEM((2, OWN_ALL, 128), F32),
            pltpu.VMEM((SCORE_H, OWN_ALL), F32),
            pltpu.VMEM((OWN_ALL, WIDTH), F32),
            pltpu.VMEM((OWN_ALL, WIDTH), F32),
            pltpu.VMEM((2, WIDTH, OWN_ALL), F32),
            pltpu.VMEM((2, OWN_ALL, WIDTH), F32),
            pltpu.VMEM((2, WIDTH, WIDTH), F32),
            pltpu.VMEM((8, 2, USERS, 128), F32),
            pltpu.VMEM((16, 2, USERS, 128), F32),
            pltpu.VMEM((8, 8, WIDTH), F32),
            pltpu.VMEM((16, 8, WIDTH), F32),
            pltpu.VMEM((2, 16, 16, WIDTH), F32),
            pltpu.VMEM((2, 16, 8, WIDTH), F32),
            pltpu.VMEM((16, 16, WIDTH), F32),
            pltpu.VMEM((16, 8, WIDTH), F32),
            pltpu.VMEM((16, 16, WIDTH), F32),
            pltpu.VMEM((16, 8, WIDTH), F32),
            pltpu.VMEM((4, 16, WIDTH), F32),
            pltpu.VMEM((4, 8, WIDTH), F32),
            dma((USERS,)),
            dma((USERS,)),
            dma((7,)),
            dma((5, USERS)),
            dma((5, USERS)),
            dma((5, USERS)),
            dma((5, USERS)),
            dma((8,)),
            dma((8,)),
            dma((16,)),
            dma((16,)),
            dma((8,)),
            dma((8,)),
            dma((16,)),
            dma((16,)),
            dma((2,)),
            dma((2,)),
            dma((2, 16)),
            dma((2, 16)),
            dma((2, 4)),
            dma((2, 4)),
            dma((2, 16)),
            dma((2, 16)),
            dma((2,)),
            dma((2,)),
        ],
        compiler_params=pltpu.CompilerParams(
            collective_id=0, has_side_effects=True, vmem_limit_bytes=62 * 1024 * 1024
        ),
        name="main_kernel",
    )(
        lengths,
        history,
        candidates,
        short_hist,
        value_weight,
        head_weight,
        pair_weight,
        event_weight,
        pooling_weight,
        itemwise_weight,
        pad_mask,
        short_mask,
        row(query_gain),
        row(head_vector),
        row(scoring_bias),
        row(weigher),
        row(hidden_bias),
        row(output_vector),
    )
    out = pl.pallas_call(
        finish_kernel,
        out_shape=(
            jax.ShapeDtypeStruct((USERS, OWN), F32),
            jax.ShapeDtypeStruct((WIDTH, SCORE_H), F32),
            jax.ShapeDtypeStruct((WIDTH, SCORE_H), F32),
            jax.ShapeDtypeStruct((1, SCORE_H), F32),
            jax.ShapeDtypeStruct((1, SCORE_H), F32),
            jax.ShapeDtypeStruct((WIDTH, WIDTH), F32),
            jax.ShapeDtypeStruct((WIDTH, WIDTH), F32),
            jax.ShapeDtypeStruct((1, WIDTH), F32),
            jax.ShapeDtypeStruct((1, WIDTH), F32),
        ),
        in_specs=[vmem] * 8,
        out_specs=(vmem,) * 9,
        name="finish_kernel",
    )(logits, mlp, att, small, pair_weight, event_weight, row(scoring_bias), row(weigher))
    flat = lambda v: v.reshape(-1)
    return (
        out[0],
        out[1],
        out[2],
        flat(out[3]),
        flat(out[4]),
        out[5],
        out[6],
        flat(out[7]),
        flat(out[8]),
    )


def solution(mesh):
    placed = (P(None, "ctx", None), P(None, "cand", None), P(), P(), P(None, "ctx")) + (P(),) * 13
    return jax.shard_map(
        body,
        mesh=mesh,
        in_specs=placed,
        out_specs=(P(None, ("cand", "ctx")),) + (P(),) * 8,
        check_vma=False,
    )
```

```python
import functools
import math

import jax
import jax.numpy as jnp
from jax import lax
from jax.experimental import pallas as pl
from jax.experimental.pallas import tpu as pltpu
from jax.sharding import PartitionSpec as P

NEG_FILL = -1e30
NEG_CLAMP = -1e29
SOFT_CAP = 10.0
F32 = jnp.float32
BF16 = jnp.bfloat16
MESH = pl.DeviceIdType.MESH

USERS = 8
CAND_DEV = 512
EVENTS = 2048
WIDTH = 256
SHORT = 256
SCORE_H = 128
OWN = 16
BLOCKS = 32
OWN_ALL = USERS * OWN
CGROUP = 4
DELAY = (5, 8, 10)
SLOTS = max(USERS + DELAY[2], 2 * USERS)
GELU_K = math.sqrt(2.0 / math.pi)
GELU_C = 0.044715


def dot(a, b, ca=1, cb=0, precision=None):
    return lax.dot_general(
        a, b, (((ca,), (cb,)), ((), ())), precision=precision, preferred_element_type=F32
    )


def halves(a):
    high = a.astype(BF16)
    return high, (a - high.astype(F32)).astype(BF16)


def dot_split(a, b, cb=0):
    n = a.shape[0]
    both = dot(jnp.concatenate(halves(a), axis=0), b, 1, cb)
    return both[:n] + both[n:]


def dot_split2(a, b, cb=0):
    n = a.shape[0]
    a_high, a_low = halves(a)
    b_high, b_low = halves(b)
    both = dot(jnp.concatenate([a_high, a_low], axis=0), b_high, 1, cb)
    return both[:n] + both[n:] + dot(a_high, b_low, 1, cb)


def gelu(p):
    return 0.5 * p * (1.0 + jnp.tanh(GELU_K * (p + GELU_C * p * p * p)))


def diag_row(col, n=128):
    lane = lax.broadcasted_iota(jnp.int32, (n, n), 1)
    sub = lax.broadcasted_iota(jnp.int32, (n, n), 0)
    return jnp.sum(jnp.where(lane == sub, jnp.broadcast_to(col, (n, n)), 0.0), axis=0, keepdims=True)


def to_column(row):
    return jnp.transpose(jnp.broadcast_to(row, (128, 128)))


def main_kernel(
    lengths,
    history,
    candidates_hbm,
    short_hbm,
    value_hbm,
    head_hbm,
    pair_hbm,
    event_hbm,
    pooling_hbm,
    itemwise_hbm,
    pad_hbm,
    mask_hbm,
    gain_hbm,
    vector_hbm,
    scoring_hbm,
    weigher_hbm,
    bias_hbm,
    output_hbm,
    logits_hbm,
    mlp_hbm,
    att_hbm,
    small_hbm,
    pad_mask,
    short_mask,
    query_gain,
    head_vector,
    scoring_bias,
    weigher,
    hidden_bias,
    output_vector,
    logits_out,
    mlp_out,
    att_out,
    small_out,
    hist,
    candidates,
    short,
    value_weight,
    head_weight,
    pair_weight,
    event_weight,
    pooling_weight,
    itemwise_weight,
    qs,
    scores,
    probs,
    inv_col,
    lse_col,
    top_part,
    top_col,
    sum_part,
    acc,
    lse,
    rv0,
    rv1,
    rv2,
    rl,
    oc,
    pw_t,
    ew_t,
    w_full,
    b_full,
    wb,
    pre,
    att,
    interest,
    dint,
    datt,
    exps,
    unit_sums,
    row_scale,
    cand_scale,
    rows_t,
    dh,
    mlp,
    st1,
    st2,
    sm1,
    sm2,
    gb0,
    gb1,
    r00,
    r01,
    r10,
    r11,
    r20,
    r21,
    hist_sem,
    cand_sem,
    load_sem,
    early_sem,
    result_sem,
    rs_vs,
    rs_vr,
    rs_ls,
    rs_lr,
    st1_s,
    st1_r,
    st2_s,
    st2_r,
    sm1_s,
    sm1_r,
    sm2_s,
    sm2_r,
    a0_s,
    a0_r,
    a1_s,
    a1_r,
    a2_s,
    a2_r,
    a3_s,
    a3_r,
    a4_s,
    a4_r,
):
    loads = (
        (short_hbm, short),
        (pair_hbm, pair_weight),
        (event_hbm, event_weight),
        (pooling_hbm, pooling_weight),
        (itemwise_hbm, itemwise_weight),
        (value_hbm, value_weight),
        (head_hbm, head_weight),
        (mask_hbm, short_mask),
        (vector_hbm, head_vector),
        (scoring_hbm, scoring_bias),
        (weigher_hbm, weigher),
        (bias_hbm, hidden_bias),
        (output_hbm, output_vector),
    )
    results = (
        (logits_out, logits_hbm),
        (mlp_out, mlp_hbm),
        (att_out, att_hbm),
        (small_out, small_hbm),
    )
    rv = (rv0, rv1, rv2)
    cand = lax.axis_index("cand")
    ctx = lax.axis_index("ctx")
    x = ctx % 4
    y_hi = (ctx // 4) % 2
    z = ctx // 8
    y_lo = cand // 2
    core = cand % 2
    y = y_hi * 2 + y_lo
    place8 = y_hi * 4 + cand
    place16 = z * 4 + x

    def peer8(k):
        return (k % 4, z * 8 + (k // 4) * 4 + x)

    def peer16(k):
        return (cand, (k // 4) * 8 + y_hi * 4 + k % 4)

    def peer_y(k):
        return ((k % 2) * 2 + core, z * 8 + (k // 2) * 4 + x)

    sibling = (y_lo * 2 + 1 - core, ctx)

    def hist_copy(u):
        return pltpu.make_async_copy(history.at[u], hist.at[u], hist_sem.at[u])

    def cand_copy(u):
        return pltpu.make_async_copy(candidates_hbm.at[u], candidates.at[u], cand_sem.at[u])

    def early(k):
        src, dst = ((pad_hbm, pad_mask), (gain_hbm, query_gain))[k]
        return pltpu.make_async_copy(src, dst, early_sem.at[k])

    def result(k):
        return pltpu.make_async_copy(results[k][0], results[k][1], result_sem.at[k])

    def load(k):
        return pltpu.make_async_copy(loads[k][0], loads[k][1], load_sem.at[k])

    for k in range(2):
        early(k).start()
    for u in range(2):
        cand_copy(u).start()
        hist_copy(u).start()
    barrier = pltpu.get_barrier_semaphore()
    for d in range(1, 8):
        pl.semaphore_signal(barrier, inc=1, device_id=peer8((place8 + d) % 8), device_id_type=MESH)
    for d in range(1, 16):
        pl.semaphore_signal(
            barrier, inc=1, device_id=peer16((place16 + d) % 16), device_id_type=MESH
        )
    for k in range(2):
        early(k).wait()

    def set_up():
        for k in range(len(loads)):
            load(k).wait()
        pw_t[...] = jnp.transpose(pair_weight[...])
        ew_t[...] = jnp.transpose(event_weight[...])
        wc = to_column(weigher[...])
        bc = to_column(scoring_bias[...])
        w_full[:, :128] = wc
        w_full[:, 128:] = wc
        b_full[:, :128] = bc
        b_full[:, 128:] = bc
        for u in range(USERS):
            oc[u] = candidates[u, pl.ds(pl.multiple_of(ctx * OWN, OWN), OWN), :].astype(F32)
        unit_sums[...] = jnp.zeros_like(unit_sums)

    stride1 = 1 + 7 * core
    stride2 = 8 - 7 * core
    c1 = (ctx // stride1) % 4
    c2 = (ctx // stride2) % 4
    stages = (
        (c1, stride1, 4, 8, 0),
        (c2, stride2, 4, 2, c1 * 8),
        (y_hi, 4, 2, 1, c1 * 8 + c2 * 2),
    )

    def rs_copies(k, u, d):
        c, stride, n, chunk, first = stages[k]
        to = (c + d) % n
        device = (cand, ctx + (to - c) * stride)
        value = pltpu.make_async_remote_copy(
            src_ref=acc.at[u, pl.ds(first + to * chunk, chunk)],
            dst_ref=rv[k].at[u, d - 1],
            send_sem=rs_vs.at[k, u, d - 1],
            recv_sem=rs_vr.at[k, u, d - 1],
            device_id=device,
            device_id_type=MESH,
        )
        weight = pltpu.make_async_remote_copy(
            src_ref=lse.at[k, u, to if k == 0 else c1],
            dst_ref=rl.at[u, 3 * k + d - 1],
            send_sem=rs_ls.at[k, u, d - 1],
            recv_sem=rs_lr.at[k, u, d - 1],
            device_id=device,
            device_id_type=MESH,
        )
        return value, weight

    def rs_send(k, u):
        for d in (2, 1, 3) if k < 2 else (1,):
            for copy in rs_copies(k, u, d):
                copy.start()

    def rs_merge(k, u):
        c, stride, n, chunk, first = stages[k]
        for d in range(1, n):
            for copy in rs_copies(k, u, d):
                copy.wait()
        logs = [lse[k, u, c1]] + [rl[u, 3 * k + d - 1] for d in range(1, n)]
        top = functools.reduce(jnp.maximum, logs)
        parts = [jnp.exp(v - top) for v in logs]
        total = functools.reduce(jnp.add, parts)
        if k < 2:
            lse[k + 1, u, c1] = top + jnp.log(total)
        shares = [jnp.concatenate([p / total] * 2, axis=0) for p in parts]
        lane = lax.broadcasted_iota(jnp.int32, (16, 128), 1)
        sub = lax.broadcasted_iota(jnp.int32, (16, 128), 0)
        for b in range(chunk):
            at = first + c * chunk + b
            here = lane - sub == (at % 8) * 16
            sum_ = None
            for j, share in enumerate(shares):
                col = jnp.sum(jnp.where(here, share, 0.0), axis=1, keepdims=True)
                term = col * (acc[u, at] if j == 0 else rv[k][u, j - 1, b])
                sum_ = term if sum_ is None else sum_ + term
            acc[u, at] = sum_

    def teacher_user(u):
        gain = query_gain[...] * (1.0 / 16.0)
        cand_copy(u).wait()
        for pos in range(BLOCKS):
            block = (pos // 8) * stride1 + (pos // 2 % 4) * stride2 + (pos % 2) * 4
            rows = candidates[u, pl.ds(pl.multiple_of(block * 16, 16), 16), :]
            qs[pos * 16 : pos * 16 + 16, :] = (rows.astype(F32) * gain).astype(BF16)
        spot = lax.broadcasted_iota(jnp.int32, (1, EVENTS), 1) + ctx * EVENTS
        ok = (spot < lengths[u]) & ((pad_mask[pl.ds(u, 1), :] == 1) | (spot == 0))
        bias = jnp.where(ok, 0.0, NEG_FILL)
        hist_copy(u).wait()
        for t in range(4):
            cols = slice(t * 512, t * 512 + 512)
            s = dot(qs[...], hist[u, cols, :], 1, 1) + bias[:, cols]
            scores[:, cols] = s
            top = s[:, :128]
            for g in range(1, 4):
                top = jnp.maximum(top, s[:, g * 128 : g * 128 + 128])
            top_part[...] = top if t == 0 else jnp.maximum(top_part[...], top)
        top = jnp.maximum(jnp.max(top_part[...], axis=1, keepdims=True), NEG_CLAMP)
        top_col[...] = jnp.broadcast_to(top, (CAND_DEV, 128))
        for r in range(16):
            rows = slice(r * 32, r * 32 + 32)
            m = top_col[rows, :]
            total = None
            for g in range(16):
                cols = slice(g * 128, g * 128 + 128)
                e = jnp.exp(scores[rows, cols] - m)
                probs[rows, cols] = e.astype(BF16)
                total = e if total is None else total + e
            sum_part[rows, :] = total
        total = jnp.sum(sum_part[...], axis=1, keepdims=True)
        some = total > 0.0
        safe = jnp.where(some, total, 1.0)
        lse_col[...] = jnp.where(some, top_col[...] + jnp.log(safe), NEG_FILL)
        inv_col[...] = jnp.broadcast_to(1.0 / safe, (CAND_DEV, 128))
        lane = lax.broadcasted_iota(jnp.int32, (128, 128), 1)
        sub = lax.broadcasted_iota(jnp.int32, (128, 128), 0)
        for g in range(4):
            rows = slice(g * 128, g * 128 + 128)
            row = jnp.sum(jnp.where(lane == sub, lse_col[rows, :], 0.0), axis=0, keepdims=True)
            lse[0, u, g] = jnp.broadcast_to(row, (8, 128))
        for t in range(2):
            rows = slice(t * 256, t * 256 + 256)
            out = dot(probs[rows, :], hist[u])
            inv = inv_col[rows, :]
            acc[u, t * 16 : t * 16 + 16, :, :128] = (out[:, :128] * inv).reshape(16, 16, 128)
            acc[u, t * 16 : t * 16 + 16, :, 128:] = (out[:, 128:] * inv).reshape(16, 16, 128)

    def short_ok(u):
        spot = lax.broadcasted_iota(jnp.int32, (1, SHORT), 1)
        return (short_mask[pl.ds(u, 1), :] == 1) | (spot == 0)

    def student_user(u):
        for cg in range(OWN // CGROUP):
            for j in range(CGROUP):
                c = cg * CGROUP + j
                w = pw_t[...] * oc[u, pl.ds(c, 1), :] + ew_t[...]
                high = w.astype(BF16)
                wb[cg, 0, j * 128 : j * 128 + 128, :] = high
                wb[cg, 1, j * 128 : j * 128 + 128, :] = (w - high.astype(F32)).astype(BF16)
            p = dot(wb[cg, 0], short[u], 1, 1) + dot(wb[cg, 1], short[u], 1, 1)
            for j in range(CGROUP):
                c = cg * CGROUP + j
                pj = p[j * 128 : j * 128 + 128, :] + b_full[...]
                pre[u, c] = pj
                att[u, pl.ds(c, 1), :] = jnp.sum(
                    jnp.maximum(pj, 0.0) * w_full[...], axis=0, keepdims=True
                )
        weights = jnp.where(short_ok(u), att[u], 0.0)
        interest[u] = dot_split(weights, short[u])

    def back_user(u):
        datt[...] = jnp.where(short_ok(u), dot_split(dint[u], short[u], 1), 0.0)
        for cg in range(OWN // CGROUP):
            cols = []
            for j in range(CGROUP):
                c = cg * CGROUP + j
                m = jnp.where(pre[u, c] > 0.0, datt[c : c + 1, :], 0.0)
                wb[cg, 0, j * 128 : j * 128 + 128, :] = m.astype(BF16)
                cols.append(jnp.sum(m, axis=1, keepdims=True))
            g = dot(wb[cg, 0], short[u])
            for j in range(CGROUP):
                pre[u, cg * CGROUP + j] = g[j * 128 : j * 128 + 128, :]
            lane = lax.broadcasted_iota(jnp.int32, (SCORE_H, OWN_ALL), 1)
            units = unit_sums[...]
            for j in range(CGROUP):
                units = jnp.where(lane == u * OWN + cg * CGROUP + j, cols[j], units)
            unit_sums[...] = units

    def reduce_steps(i):
        for k in reversed(range(3)):
            u = i - DELAY[k]

            def step(k=k, u=u):
                rs_merge(k, u)
                if k < 2:
                    rs_send(k + 1, u)

            pl.when((u >= 0) & (u < USERS))(step)

    def teacher_slot(i, carry):
        @pl.when(i + 2 < USERS)
        def _():
            cand_copy(i + 2).start()
            hist_copy(i + 2).start()

        @pl.when(i == USERS - 2)
        def _():
            for k in range(len(loads)):
                load(k).start()

        teacher_user(i)

        @pl.when(i == 0)
        def _():
            pl.semaphore_wait(barrier, 22)

        rs_send(0, i)
        reduce_steps(i)
        return carry

    lax.fori_loop(0, USERS, teacher_slot, 0)
    set_up()

    def student_slot(i, carry):
        student_user(i - USERS)
        reduce_steps(i)
        return carry

    lax.fori_loop(USERS, 2 * USERS, student_slot, 0)

    own_all = oc[...].reshape(OWN_ALL, WIDTH)
    inter = interest[...].reshape(OWN_ALL, WIDTH)
    hid = (
        dot_split2(inter, pooling_weight[...])
        + dot_split2(own_all, itemwise_weight[...])
        + hidden_bias[...]
    )
    th = jnp.tanh(GELU_K * (hid + GELU_C * hid * hid * hid))
    s_hidden = 0.5 * hid * (1.0 + th)
    slope = 0.5 * (1.0 + th) + 0.5 * hid * (1.0 - th * th) * (
        GELU_K * (1.0 + 3.0 * GELU_C * hid * hid)
    )
    s_tanh = jnp.tanh(jnp.sum(s_hidden * output_vector[...], axis=1, keepdims=True) / SOFT_CAP)
    draw = 1.0 - s_tanh * s_tanh
    dhid = draw * output_vector[...] * slope
    dinter = dot_split2(dhid, pooling_weight[...], 1)
    dint[...] = dinter.reshape(USERS, OWN, WIDTH)
    dh[0] = dhid
    dh[1] = s_hidden * draw
    s_exp = jnp.broadcast_to(jnp.exp(SOFT_CAP * s_tanh), (OWN_ALL, 128))
    exps[0] = s_exp
    rows_t[0] = jnp.transpose(inter)
    rows_t[1] = jnp.transpose(own_all)

    def back_slot(i, carry):
        back_user(i - 2 * USERS)
        reduce_steps(i)
        return carry

    lax.fori_loop(2 * USERS, SLOTS, back_slot, 0)

    own_all = oc[...].reshape(OWN_ALL, WIDTH)
    parts = []
    for u in range(USERS):
        parts.append(acc[u, c1 * 8 + c2 * 2 + y_hi])
    pooled = dot_split(jnp.concatenate(parts, axis=0), value_weight[...])
    normed = pooled * lax.rsqrt(jnp.mean(pooled * pooled, axis=1, keepdims=True) + 1e-6)
    mixed = (normed * own_all).astype(BF16)
    t_hidden = gelu(dot(mixed, head_weight[...]))
    t_logit = SOFT_CAP * jnp.tanh(
        jnp.sum(t_hidden * head_vector[...], axis=1, keepdims=True) / SOFT_CAP
    )
    lane = lax.broadcasted_iota(jnp.int32, (OWN_ALL, 128), 1)
    sub = lax.broadcasted_iota(jnp.int32, (OWN_ALL, 128), 0)
    logits_out[...] = jnp.sum(
        jnp.where(lane == sub % OWN, jnp.broadcast_to(t_logit, (OWN_ALL, 128)), 0.0).reshape(
            USERS, OWN, 128
        ),
        axis=1,
    )

    result(0).start()

    t_exp = jnp.broadcast_to(jnp.exp(t_logit), (OWN_ALL, 128))
    exps[1] = t_exp

    def exchange(slots, count, me, peer, send_sem, recv_sem):
        def copy(k, to):
            return pltpu.make_async_remote_copy(
                src_ref=slots.at[me],
                dst_ref=slots.at[me],
                send_sem=send_sem.at[k],
                recv_sem=recv_sem.at[me],
                device_id=to,
                device_id_type=MESH,
            )

        def arrival(k):
            return pltpu.make_async_remote_copy(
                src_ref=slots.at[me],
                dst_ref=slots.at[k],
                send_sem=send_sem.at[k],
                recv_sem=recv_sem.at[k],
                device_id=peer(k),
                device_id_type=MESH,
            )

        def start():
            for d in range(1, count):
                k = (me + d) % count
                copy(k, peer(k)).start()

        def wait():
            for d in range(1, count):
                k = (me + d) % count
                arrival(k).wait_recv()
            for d in range(1, count):
                k = (me + d) % count
                copy(k, peer(k)).wait_send()

        return start, wait

    st1[place8, 0] = jnp.sum(exps[0].reshape(USERS, OWN, 128), axis=1)
    st1[place8, 1] = jnp.sum(t_exp.reshape(USERS, OWN, 128), axis=1)

    def more_back(first, last):
        def one(u, carry):
            back_user(u)
            return carry

        lax.fori_loop(first, last, one, 0)

    done = SLOTS - 2 * USERS
    start, wait = exchange(st1, 8, place8, peer8, st1_s, st1_r)
    start()
    more_back(done, (done + USERS) // 2)
    wait()
    st2[place16] = jnp.sum(st1[...], axis=0)
    start, wait = exchange(st2, 16, place16, peer16, st2_s, st2_r)
    start()
    more_back((done + USERS) // 2, USERS)
    wait()
    sums = jnp.sum(st2[...], axis=0)

    def wide(v):
        return jnp.broadcast_to(v[:, None, :], (USERS, OWN, 128)).reshape(OWN_ALL, 128)

    scale = math.sqrt(4 * CAND_DEV / USERS)
    logit_grad = scale * (exps[0] / wide(sums[0]) - exps[1] / wide(sums[1]))
    row_scale[:, :128] = logit_grad
    row_scale[:, 128:] = logit_grad
    cand_scale[...] = row_scale[...] * oc[...].reshape(OWN_ALL, WIDTH)
    dh[0] = dh[0] * row_scale[...]
    dh[1] = dh[1] * row_scale[...]

    def mlp_half(h, carry):
        mlp[h] = dot_split2(rows_t[h], dh[0])
        return carry

    lax.fori_loop(0, 2, mlp_half, 0)

    others = [(place16 + d) % 16 for d in range(1, 16)]

    def all_reduce(n, gb, r0, r1, r2, out):
        def swap():
            return pltpu.make_async_remote_copy(
                src_ref=gb.at[1 - core],
                dst_ref=r0,
                send_sem=a0_s.at[n],
                recv_sem=a0_r.at[n],
                device_id=sibling,
                device_id_type=MESH,
            )

        def scatter(k, slot):
            return pltpu.make_async_remote_copy(
                src_ref=r0.at[k],
                dst_ref=r1.at[slot],
                send_sem=a1_s.at[n, k],
                recv_sem=a1_r.at[n, slot],
                device_id=peer16(k),
                device_id_type=MESH,
            )

        def spread(k, slot):
            return pltpu.make_async_remote_copy(
                src_ref=out.at[core, slot],
                dst_ref=out.at[core, slot],
                send_sem=a3_s.at[n, k],
                recv_sem=a3_r.at[n, slot],
                device_id=peer16(k),
                device_id_type=MESH,
            )

        def last(slot):
            return pltpu.make_async_remote_copy(
                src_ref=out.at[core],
                dst_ref=out.at[slot],
                send_sem=a4_s.at[n],
                recv_sem=a4_r.at[n],
                device_id=sibling,
                device_id_type=MESH,
            )

        start_y, wait_y = exchange(r2, 4, y, peer_y, a2_s.at[n], a2_r.at[n])

        def step0():
            swap().start()

        def step1():
            swap().wait()
            r0[...] = r0[...] + gb[core]
            for k in others:
                scatter(k, place16).start()
            r1[place16] = r0[place16]

        def step2():
            for k in others:
                scatter(k, k).wait_recv()
            r2[y] = jnp.sum(r1[...], axis=0)
            start_y()

        def step3():
            wait_y()
            out[core, place16] = jnp.sum(r2[...], axis=0)
            for k in others:
                spread(k, place16).start()

        def step4():
            for k in others:
                spread(k, k).wait_recv()
            last(core).start()

        def step5():
            for k in others:
                scatter(k, place16).wait_send()
                spread(k, place16).wait_send()
            last(core).wait_send()
            last(1 - core).wait_recv()

        return step0, step1, step2, step3, step4, step5

    first = all_reduce(0, gb0, r00, r10, r20, mlp_out)
    second = all_reduce(1, gb1, r01, r11, r21, att_out)
    for h in range(2):
        gb0[h] = mlp[h].reshape(16, 16, WIDTH)
    first[0]()

    for ab in range(2):
        rows = slice(ab * 64, ab * 64 + 64)

        def add(i, carry):
            p, e = carry
            for j in range(OWN):
                g = pre[i, j, rows, :]
                p = p + g * cand_scale[pl.ds(i * OWN + j, 1), :]
                e = e + g * row_scale[pl.ds(i * OWN + j, 1), :]
            return p, e

        zero = jnp.zeros((64, WIDTH), F32)
        p, e = lax.fori_loop(0, USERS, add, (zero, zero))
        gb1[0, ab * 8 : ab * 8 + 8] = p.reshape(8, 8, WIDTH)
        gb1[1, ab * 8 : ab * 8 + 8] = e.reshape(8, 8, WIDTH)
        if ab == 0:
            first[1]()
    second[0]()
    lane = lax.broadcasted_iota(jnp.int32, (OWN_ALL, 128), 1)
    sub = lax.broadcasted_iota(jnp.int32, (OWN_ALL, 128), 0)
    scale_row = diag_row(row_scale[:, :128])
    g_row = diag_row(jnp.sum(unit_sums[...] * scale_row, axis=1, keepdims=True))
    sm1[place8] = jnp.concatenate(
        [
            jnp.concatenate([g_row, jnp.zeros_like(g_row)], axis=1),
            jnp.sum(dh[0], axis=0, keepdims=True),
            jnp.sum(dh[1], axis=0, keepdims=True),
            jnp.zeros((5, WIDTH), F32),
        ],
        axis=0,
    )
    start, wait = exchange(sm1, 8, place8, peer8, sm1_s, sm1_r)
    start()
    second[1]()
    first[2]()
    wait()
    sm2[place16] = jnp.sum(sm1[...], axis=0)
    start, wait = exchange(sm2, 16, place16, peer16, sm2_s, sm2_r)
    start()
    second[2]()
    first[3]()
    second[3]()
    wait()
    small_out[...] = jnp.sum(sm2[...], axis=0)
    result(3).start()
    first[4]()
    second[4]()
    first[5]()
    result(1).start()
    second[5]()
    result(2).start()
    for k in range(4):
        result(k).wait()


def finish_kernel(
    logits,
    mlp,
    att,
    small,
    pair_weight,
    event_weight,
    scoring_bias,
    weigher,
    logits_out,
    pair_out,
    event_out,
    scoring_out,
    weigher_out,
    pooling_out,
    itemwise_out,
    hidden_out,
    output_out,
):
    flat = mlp[...].reshape(512, WIDTH)
    attention = att[...].reshape(256, WIDTH)
    w = weigher[...]
    pair = jnp.transpose(attention[:128])
    event = jnp.transpose(attention[128:])
    g = small[0:1, :128]
    pair_out[...] = pair * w
    event_out[...] = event * w
    scoring_out[...] = g * w
    weigher_out[...] = scoring_bias[...] * g + jnp.sum(
        pair * pair_weight[...] + event * event_weight[...], axis=0, keepdims=True
    )
    pooling_out[...] = flat[:256]
    itemwise_out[...] = flat[256:]
    hidden_out[...] = small[1:2, :]
    output_out[...] = small[2:3, :]
    logits_out[...] = logits[:, :OWN]


def body(
    history,
    candidates,
    short_hist,
    lengths,
    pad_mask,
    short_mask,
    query_gain,
    value_weight,
    head_weight,
    head_vector,
    pair_weight,
    event_weight,
    scoring_bias,
    weigher,
    pooling_weight,
    itemwise_weight,
    hidden_bias,
    output_vector,
):
    vmem = pl.BlockSpec(memory_space=pltpu.VMEM)
    row = lambda v: v.reshape(1, -1)
    dma = pltpu.SemaphoreType.DMA
    logits, mlp, att, small = pl.pallas_call(
        main_kernel,
        out_shape=(
            jax.ShapeDtypeStruct((USERS, 128), F32),
            jax.ShapeDtypeStruct((2, 16, 16, WIDTH), F32),
            jax.ShapeDtypeStruct((2, 16, 8, WIDTH), F32),
            jax.ShapeDtypeStruct((8, WIDTH), F32),
        ),
        in_specs=[
            pl.BlockSpec(memory_space=pltpu.SMEM),
        ]
        + [pl.BlockSpec(memory_space=pl.ANY)] * 17,
        out_specs=(pl.BlockSpec(memory_space=pl.ANY),) * 4,
        scratch_shapes=[
            pltpu.VMEM((USERS, EVENTS), jnp.int32),
            pltpu.VMEM((USERS, SHORT), jnp.int32),
            pltpu.VMEM((1, WIDTH), F32),
            pltpu.VMEM((1, WIDTH), F32),
            pltpu.VMEM((1, SCORE_H), F32),
            pltpu.VMEM((1, SCORE_H), F32),
            pltpu.VMEM((1, WIDTH), F32),
            pltpu.VMEM((1, WIDTH), F32),
            pltpu.VMEM((USERS, 128), F32),
            pltpu.VMEM((2, 16, 16, WIDTH), F32),
            pltpu.VMEM((2, 16, 8, WIDTH), F32),
            pltpu.VMEM((8, WIDTH), F32),
            pltpu.VMEM((USERS, EVENTS, WIDTH), BF16),
            pltpu.VMEM((USERS, CAND_DEV, WIDTH), BF16),
            pltpu.VMEM((USERS, SHORT, WIDTH), BF16),
            pltpu.VMEM((WIDTH, WIDTH), BF16),
            pltpu.VMEM((WIDTH, WIDTH), BF16),
            pltpu.VMEM((WIDTH, SCORE_H), F32),
            pltpu.VMEM((WIDTH, SCORE_H), F32),
            pltpu.VMEM((WIDTH, WIDTH), F32),
            pltpu.VMEM((WIDTH, WIDTH), F32),
            pltpu.VMEM((CAND_DEV, WIDTH), BF16),
            pltpu.VMEM((CAND_DEV, EVENTS), F32),
            pltpu.VMEM((CAND_DEV, EVENTS), BF16),
            pltpu.VMEM((CAND_DEV, 128), F32),
            pltpu.VMEM((CAND_DEV, 128), F32),
            pltpu.VMEM((CAND_DEV, 128), F32),
            pltpu.VMEM((CAND_DEV, 128), F32),
            pltpu.VMEM((CAND_DEV, 128), F32),
            pltpu.VMEM((USERS, BLOCKS, OWN, WIDTH), F32),
            pltpu.VMEM((3, USERS, 4, 8, 128), F32),
            pltpu.VMEM((USERS, 3, 8, OWN, WIDTH), F32),
            pltpu.VMEM((USERS, 3, 2, OWN, WIDTH), F32),
            pltpu.VMEM((USERS, 1, 1, OWN, WIDTH), F32),
            pltpu.VMEM((USERS, 7, 8, 128), F32),
            pltpu.VMEM((USERS, OWN, WIDTH), F32),
            pltpu.VMEM((SCORE_H, WIDTH), F32),
            pltpu.VMEM((SCORE_H, WIDTH), F32),
            pltpu.VMEM((SCORE_H, WIDTH), F32),
            pltpu.VMEM((SCORE_H, WIDTH), F32),
            pltpu.VMEM((OWN // CGROUP, 2, CGROUP * SCORE_H, WIDTH), BF16),
            pltpu.VMEM((USERS, OWN, SCORE_H, SHORT), F32),
            pltpu.VMEM((USERS, OWN, SHORT), F32),
            pltpu.VMEM((USERS, OWN, WIDTH), F32),
            pltpu.VMEM((USERS, OWN, WIDTH), F32),
            pltpu.VMEM((OWN, SHORT), F32),
            pltpu.VMEM((2, OWN_ALL, 128), F32),
            pltpu.VMEM((SCORE_H, OWN_ALL), F32),
            pltpu.VMEM((OWN_ALL, WIDTH), F32),
            pltpu.VMEM((OWN_ALL, WIDTH), F32),
            pltpu.VMEM((2, WIDTH, OWN_ALL), F32),
            pltpu.VMEM((2, OWN_ALL, WIDTH), F32),
            pltpu.VMEM((2, WIDTH, WIDTH), F32),
            pltpu.VMEM((8, 2, USERS, 128), F32),
            pltpu.VMEM((16, 2, USERS, 128), F32),
            pltpu.VMEM((8, 8, WIDTH), F32),
            pltpu.VMEM((16, 8, WIDTH), F32),
            pltpu.VMEM((2, 16, 16, WIDTH), F32),
            pltpu.VMEM((2, 16, 8, WIDTH), F32),
            pltpu.VMEM((16, 16, WIDTH), F32),
            pltpu.VMEM((16, 8, WIDTH), F32),
            pltpu.VMEM((16, 16, WIDTH), F32),
            pltpu.VMEM((16, 8, WIDTH), F32),
            pltpu.VMEM((4, 16, WIDTH), F32),
            pltpu.VMEM((4, 8, WIDTH), F32),
            dma((USERS,)),
            dma((USERS,)),
            dma((13,)),
            dma((2,)),
            dma((4,)),
            dma((3, USERS, 3)),
            dma((3, USERS, 3)),
            dma((3, USERS, 3)),
            dma((3, USERS, 3)),
            dma((8,)),
            dma((8,)),
            dma((16,)),
            dma((16,)),
            dma((8,)),
            dma((8,)),
            dma((16,)),
            dma((16,)),
            dma((2,)),
            dma((2,)),
            dma((2, 16)),
            dma((2, 16)),
            dma((2, 4)),
            dma((2, 4)),
            dma((2, 16)),
            dma((2, 16)),
            dma((2,)),
            dma((2,)),
        ],
        compiler_params=pltpu.CompilerParams(
            collective_id=0, has_side_effects=True, vmem_limit_bytes=62 * 1024 * 1024
        ),
        name="main_kernel",
    )(
        lengths,
        history,
        candidates,
        short_hist,
        value_weight,
        head_weight,
        pair_weight,
        event_weight,
        pooling_weight,
        itemwise_weight,
        pad_mask,
        short_mask,
        row(query_gain),
        row(head_vector),
        row(scoring_bias),
        row(weigher),
        row(hidden_bias),
        row(output_vector),
    )
    out = pl.pallas_call(
        finish_kernel,
        out_shape=(
            jax.ShapeDtypeStruct((USERS, OWN), F32),
            jax.ShapeDtypeStruct((WIDTH, SCORE_H), F32),
            jax.ShapeDtypeStruct((WIDTH, SCORE_H), F32),
            jax.ShapeDtypeStruct((1, SCORE_H), F32),
            jax.ShapeDtypeStruct((1, SCORE_H), F32),
            jax.ShapeDtypeStruct((WIDTH, WIDTH), F32),
            jax.ShapeDtypeStruct((WIDTH, WIDTH), F32),
            jax.ShapeDtypeStruct((1, WIDTH), F32),
            jax.ShapeDtypeStruct((1, WIDTH), F32),
        ),
        in_specs=[vmem] * 8,
        out_specs=(vmem,) * 9,
        name="finish_kernel",
    )(logits, mlp, att, small, pair_weight, event_weight, row(scoring_bias), row(weigher))
    flat = lambda v: v.reshape(-1)
    return (
        out[0],
        out[1],
        out[2],
        flat(out[3]),
        flat(out[4]),
        out[5],
        out[6],
        flat(out[7]),
        flat(out[8]),
    )


def solution(mesh):
    placed = (P(None, "ctx", None), P(None, "cand", None), P(), P(), P(None, "ctx")) + (P(),) * 13
    return jax.shard_map(
        body,
        mesh=mesh,
        in_specs=placed,
        out_specs=(P(None, ("cand", "ctx")),) + (P(),) * 8,
        check_vma=False,
    )
```

```python
import functools
import math

import jax
import jax.numpy as jnp
from jax import lax
from jax.experimental import pallas as pl
from jax.experimental.pallas import tpu as pltpu
from jax.sharding import PartitionSpec as P

NEG_FILL = -1e30
NEG_CLAMP = -1e29
SOFT_CAP = 10.0
F32 = jnp.float32
BF16 = jnp.bfloat16
MESH = pl.DeviceIdType.MESH

USERS = 8
CAND_DEV = 512
EVENTS = 2048
WIDTH = 256
SHORT = 256
SCORE_H = 128
OWN = 16
BLOCKS = 32
OWN_ALL = USERS * OWN
CGROUP = 4
DELAY = (5, 8, 10)
SLOTS = max(USERS + DELAY[2], 2 * USERS)
GELU_K = math.sqrt(2.0 / math.pi)
GELU_C = 0.044715


def dot(a, b, ca=1, cb=0, precision=None):
    return lax.dot_general(
        a, b, (((ca,), (cb,)), ((), ())), precision=precision, preferred_element_type=F32
    )


def halves(a):
    high = a.astype(BF16)
    return high, (a - high.astype(F32)).astype(BF16)


def dot_split(a, b, cb=0):
    n = a.shape[0]
    both = dot(jnp.concatenate(halves(a), axis=0), b, 1, cb)
    return both[:n] + both[n:]


def dot_split2(a, b, cb=0):
    n = a.shape[0]
    a_high, a_low = halves(a)
    b_high, b_low = halves(b)
    both = dot(jnp.concatenate([a_high, a_low], axis=0), b_high, 1, cb)
    return both[:n] + both[n:] + dot(a_high, b_low, 1, cb)


def gelu(p):
    return 0.5 * p * (1.0 + jnp.tanh(GELU_K * (p + GELU_C * p * p * p)))


def diag_row(col, n=128):
    lane = lax.broadcasted_iota(jnp.int32, (n, n), 1)
    sub = lax.broadcasted_iota(jnp.int32, (n, n), 0)
    return jnp.sum(jnp.where(lane == sub, jnp.broadcast_to(col, (n, n)), 0.0), axis=0, keepdims=True)


def to_column(row):
    return jnp.transpose(jnp.broadcast_to(row, (128, 128)))


def main_kernel(
    lengths,
    history,
    candidates_hbm,
    short_hbm,
    value_hbm,
    head_hbm,
    pair_hbm,
    event_hbm,
    pooling_hbm,
    itemwise_hbm,
    pad_hbm,
    mask_hbm,
    gain_hbm,
    vector_hbm,
    scoring_hbm,
    weigher_hbm,
    bias_hbm,
    output_hbm,
    logits_hbm,
    mlp_hbm,
    att_hbm,
    small_hbm,
    pad_mask,
    short_mask,
    query_gain,
    head_vector,
    scoring_bias,
    weigher,
    hidden_bias,
    output_vector,
    logits_out,
    mlp_out,
    att_out,
    small_out,
    hist,
    candidates,
    short,
    value_weight,
    head_weight,
    pair_weight,
    event_weight,
    pooling_weight,
    itemwise_weight,
    qs,
    scores,
    probs,
    inv_col,
    lse_col,
    top_part,
    top_col,
    sum_part,
    acc,
    lse,
    rv0,
    rv1,
    rv2,
    rl,
    oc,
    pw_t,
    ew_t,
    w_full,
    b_full,
    wb,
    pre,
    att,
    interest,
    dint,
    datt,
    exps,
    unit_sums,
    row_scale,
    cand_scale,
    rows_t,
    dh,
    mlp,
    st1,
    st2,
    sm1,
    sm2,
    gb0,
    gb1,
    r00,
    r01,
    r10,
    r11,
    r20,
    r21,
    hist_sem,
    cand_sem,
    load_sem,
    early_sem,
    result_sem,
    rs_vs,
    rs_vr,
    rs_ls,
    rs_lr,
    st1_s,
    st1_r,
    st2_s,
    st2_r,
    sm1_s,
    sm1_r,
    sm2_s,
    sm2_r,
    a0_s,
    a0_r,
    a1_s,
    a1_r,
    a2_s,
    a2_r,
    a3_s,
    a3_r,
    a4_s,
    a4_r,
):
    loads = (
        (short_hbm, short),
        (pair_hbm, pair_weight),
        (event_hbm, event_weight),
        (pooling_hbm, pooling_weight),
        (itemwise_hbm, itemwise_weight),
        (value_hbm, value_weight),
        (head_hbm, head_weight),
        (mask_hbm, short_mask),
        (vector_hbm, head_vector),
        (scoring_hbm, scoring_bias),
        (weigher_hbm, weigher),
        (bias_hbm, hidden_bias),
        (output_hbm, output_vector),
    )
    results = (
        (logits_out, logits_hbm),
        (mlp_out, mlp_hbm),
        (att_out, att_hbm),
        (small_out, small_hbm),
    )
    rv = (rv0, rv1, rv2)
    cand = lax.axis_index("cand")
    ctx = lax.axis_index("ctx")
    x = ctx % 4
    y_hi = (ctx // 4) % 2
    z = ctx // 8
    y_lo = cand // 2
    core = cand % 2
    y = y_hi * 2 + y_lo
    place8 = y_hi * 4 + cand
    place16 = z * 4 + x

    def peer8(k):
        return (k % 4, z * 8 + (k // 4) * 4 + x)

    def peer16(k):
        return (cand, (k // 4) * 8 + y_hi * 4 + k % 4)

    def peer_y(k):
        return ((k % 2) * 2 + core, z * 8 + (k // 2) * 4 + x)

    sibling = (y_lo * 2 + 1 - core, ctx)

    def hist_copy(u):
        return pltpu.make_async_copy(history.at[u], hist.at[u], hist_sem.at[u])

    def cand_copy(u):
        return pltpu.make_async_copy(candidates_hbm.at[u], candidates.at[u], cand_sem.at[u])

    def early(k):
        src, dst = ((pad_hbm, pad_mask), (gain_hbm, query_gain))[k]
        return pltpu.make_async_copy(src, dst, early_sem.at[k])

    def result(k):
        return pltpu.make_async_copy(results[k][0], results[k][1], result_sem.at[k])

    def load(k):
        return pltpu.make_async_copy(loads[k][0], loads[k][1], load_sem.at[k])

    for k in range(2):
        early(k).start()
    for u in range(2):
        cand_copy(u).start()
        hist_copy(u).start()
    barrier = pltpu.get_barrier_semaphore()
    for d in range(1, 8):
        pl.semaphore_signal(barrier, inc=1, device_id=peer8((place8 + d) % 8), device_id_type=MESH)
    for d in range(1, 16):
        pl.semaphore_signal(
            barrier, inc=1, device_id=peer16((place16 + d) % 16), device_id_type=MESH
        )
    for k in range(2):
        early(k).wait()

    def set_up():
        for k in range(len(loads)):
            load(k).wait()
        pw_t[...] = jnp.transpose(pair_weight[...])
        ew_t[...] = jnp.transpose(event_weight[...])
        wc = to_column(weigher[...])
        bc = to_column(scoring_bias[...])
        w_full[:, :128] = wc
        w_full[:, 128:] = wc
        b_full[:, :128] = bc
        b_full[:, 128:] = bc
        for u in range(USERS):
            oc[u] = candidates[u, pl.ds(pl.multiple_of(ctx * OWN, OWN), OWN), :].astype(F32)
        unit_sums[...] = jnp.zeros_like(unit_sums)

    stride1 = 1 + 7 * core
    stride2 = 8 - 7 * core
    c1 = (ctx // stride1) % 4
    c2 = (ctx // stride2) % 4
    stages = (
        (c1, stride1, 4, 8, 0),
        (c2, stride2, 4, 2, c1 * 8),
        (y_hi, 4, 2, 1, c1 * 8 + c2 * 2),
    )

    def rs_copies(k, u, d):
        c, stride, n, chunk, first = stages[k]
        to = (c + d) % n
        device = (cand, ctx + (to - c) * stride)
        value = pltpu.make_async_remote_copy(
            src_ref=acc.at[u, pl.ds(first + to * chunk, chunk)],
            dst_ref=rv[k].at[u, d - 1],
            send_sem=rs_vs.at[k, u, d - 1],
            recv_sem=rs_vr.at[k, u, d - 1],
            device_id=device,
            device_id_type=MESH,
        )
        weight = pltpu.make_async_remote_copy(
            src_ref=lse.at[k, u, to if k == 0 else c1],
            dst_ref=rl.at[u, 3 * k + d - 1],
            send_sem=rs_ls.at[k, u, d - 1],
            recv_sem=rs_lr.at[k, u, d - 1],
            device_id=device,
            device_id_type=MESH,
        )
        return value, weight

    def rs_send(k, u):
        for d in (2, 1, 3) if k < 2 else (1,):
            for copy in rs_copies(k, u, d):
                copy.start()

    def rs_merge(k, u):
        c, stride, n, chunk, first = stages[k]
        for d in range(1, n):
            for copy in rs_copies(k, u, d):
                copy.wait()
        logs = [lse[k, u, c1]] + [rl[u, 3 * k + d - 1] for d in range(1, n)]
        top = functools.reduce(jnp.maximum, logs)
        parts = [jnp.exp(v - top) for v in logs]
        total = functools.reduce(jnp.add, parts)
        if k < 2:
            lse[k + 1, u, c1] = top + jnp.log(total)
        shares = [jnp.concatenate([p / total] * 2, axis=0) for p in parts]
        lane = lax.broadcasted_iota(jnp.int32, (16, 128), 1)
        sub = lax.broadcasted_iota(jnp.int32, (16, 128), 0)
        for b in range(chunk):
            at = first + c * chunk + b
            here = lane - sub == (at % 8) * 16
            sum_ = None
            for j, share in enumerate(shares):
                col = jnp.sum(jnp.where(here, share, 0.0), axis=1, keepdims=True)
                term = col * (acc[u, at] if j == 0 else rv[k][u, j - 1, b])
                sum_ = term if sum_ is None else sum_ + term
            acc[u, at] = sum_

    def teacher_user(u):
        gain = query_gain[...] * (1.0 / 16.0)
        cand_copy(u).wait()
        for pos in range(BLOCKS):
            block = (pos // 8) * stride1 + (pos // 2 % 4) * stride2 + (pos % 2) * 4
            rows = candidates[u, pl.ds(pl.multiple_of(block * 16, 16), 16), :]
            qs[pos * 16 : pos * 16 + 16, :] = (rows.astype(F32) * gain).astype(BF16)
        spot = lax.broadcasted_iota(jnp.int32, (1, EVENTS), 1) + ctx * EVENTS
        ok = (spot < lengths[u]) & ((pad_mask[pl.ds(u, 1), :] == 1) | (spot == 0))
        bias = jnp.where(ok, 0.0, NEG_FILL)
        hist_copy(u).wait()
        for t in range(4):
            cols = slice(t * 512, t * 512 + 512)
            s = dot(qs[...], hist[u, cols, :], 1, 1) + bias[:, cols]
            scores[:, cols] = s
            top = s[:, :128]
            for g in range(1, 4):
                top = jnp.maximum(top, s[:, g * 128 : g * 128 + 128])
            top_part[...] = top if t == 0 else jnp.maximum(top_part[...], top)
        top = jnp.maximum(jnp.max(top_part[...], axis=1, keepdims=True), NEG_CLAMP)
        top_col[...] = jnp.broadcast_to(top, (CAND_DEV, 128))
        for r in range(16):
            rows = slice(r * 32, r * 32 + 32)
            m = top_col[rows, :]
            total = None
            for g in range(16):
                cols = slice(g * 128, g * 128 + 128)
                e = jnp.exp(scores[rows, cols] - m)
                probs[rows, cols] = e.astype(BF16)
                total = e if total is None else total + e
            sum_part[rows, :] = total
        total = jnp.sum(sum_part[...], axis=1, keepdims=True)
        some = total > 0.0
        safe = jnp.where(some, total, 1.0)
        lse_col[...] = jnp.where(some, top_col[...] + jnp.log(safe), NEG_FILL)
        inv_col[...] = jnp.broadcast_to(1.0 / safe, (CAND_DEV, 128))
        lane = lax.broadcasted_iota(jnp.int32, (128, 128), 1)
        sub = lax.broadcasted_iota(jnp.int32, (128, 128), 0)
        for g in range(4):
            rows = slice(g * 128, g * 128 + 128)
            row = jnp.sum(jnp.where(lane == sub, lse_col[rows, :], 0.0), axis=0, keepdims=True)
            lse[0, u, g] = jnp.broadcast_to(row, (8, 128))
        for t in range(2):
            rows = slice(t * 256, t * 256 + 256)
            out = dot(probs[rows, :], hist[u])
            inv = inv_col[rows, :]
            acc[u, t * 16 : t * 16 + 16, :, :128] = (out[:, :128] * inv).reshape(16, 16, 128)
            acc[u, t * 16 : t * 16 + 16, :, 128:] = (out[:, 128:] * inv).reshape(16, 16, 128)

    def short_ok(u):
        spot = lax.broadcasted_iota(jnp.int32, (1, SHORT), 1)
        return (short_mask[pl.ds(u, 1), :] == 1) | (spot == 0)

    def student_user(u):
        for cg in range(OWN // CGROUP):
            for j in range(CGROUP):
                c = cg * CGROUP + j
                w = pw_t[...] * oc[u, pl.ds(c, 1), :] + ew_t[...]
                high = w.astype(BF16)
                wb[cg, 0, j * 128 : j * 128 + 128, :] = high
                wb[cg, 1, j * 128 : j * 128 + 128, :] = (w - high.astype(F32)).astype(BF16)
            p = dot(wb[cg, 0], short[u], 1, 1) + dot(wb[cg, 1], short[u], 1, 1)
            for j in range(CGROUP):
                c = cg * CGROUP + j
                pj = p[j * 128 : j * 128 + 128, :] + b_full[...]
                pre[u, c] = pj
                att[u, pl.ds(c, 1), :] = jnp.sum(
                    jnp.maximum(pj, 0.0) * w_full[...], axis=0, keepdims=True
                )
        weights = jnp.where(short_ok(u), att[u], 0.0)
        interest[u] = dot_split(weights, short[u])

    def back_user(u):
        datt[...] = jnp.where(short_ok(u), dot_split(dint[u], short[u], 1), 0.0)
        for cg in range(OWN // CGROUP):
            cols = []
            for j in range(CGROUP):
                c = cg * CGROUP + j
                m = jnp.where(pre[u, c] > 0.0, datt[c : c + 1, :], 0.0)
                wb[cg, 0, j * 128 : j * 128 + 128, :] = m.astype(BF16)
                cols.append(jnp.sum(m, axis=1, keepdims=True))
            g = dot(wb[cg, 0], short[u])
            for j in range(CGROUP):
                pre[u, cg * CGROUP + j] = g[j * 128 : j * 128 + 128, :]
            lane = lax.broadcasted_iota(jnp.int32, (SCORE_H, OWN_ALL), 1)
            units = unit_sums[...]
            for j in range(CGROUP):
                units = jnp.where(lane == u * OWN + cg * CGROUP + j, cols[j], units)
            unit_sums[...] = units

    def reduce_steps(i):
        for k in reversed(range(3)):
            u = i - DELAY[k]

            def step(k=k, u=u):
                rs_merge(k, u)
                if k < 2:
                    rs_send(k + 1, u)

            pl.when((u >= 0) & (u < USERS))(step)

    def teacher_slot(i, carry):
        @pl.when(i + 2 < USERS)
        def _():
            cand_copy(i + 2).start()
            hist_copy(i + 2).start()

        @pl.when(i == USERS - 2)
        def _():
            for k in range(len(loads)):
                load(k).start()

        teacher_user(i)

        @pl.when(i == 0)
        def _():
            pl.semaphore_wait(barrier, 22)

        rs_send(0, i)
        reduce_steps(i)
        return carry

    lax.fori_loop(0, USERS, teacher_slot, 0)
    set_up()

    def student_slot(i, carry):
        student_user(i - USERS)
        reduce_steps(i)
        return carry

    lax.fori_loop(USERS, 2 * USERS, student_slot, 0)

    own_all = oc[...].reshape(OWN_ALL, WIDTH)
    inter = interest[...].reshape(OWN_ALL, WIDTH)
    hid = (
        dot_split2(inter, pooling_weight[...])
        + dot_split2(own_all, itemwise_weight[...])
        + hidden_bias[...]
    )
    th = jnp.tanh(GELU_K * (hid + GELU_C * hid * hid * hid))
    s_hidden = 0.5 * hid * (1.0 + th)
    slope = 0.5 * (1.0 + th) + 0.5 * hid * (1.0 - th * th) * (
        GELU_K * (1.0 + 3.0 * GELU_C * hid * hid)
    )
    s_tanh = jnp.tanh(jnp.sum(s_hidden * output_vector[...], axis=1, keepdims=True) / SOFT_CAP)
    draw = 1.0 - s_tanh * s_tanh
    dhid = draw * output_vector[...] * slope
    dinter = dot_split2(dhid, pooling_weight[...], 1)
    dint[...] = dinter.reshape(USERS, OWN, WIDTH)
    dh[0] = dhid
    dh[1] = s_hidden * draw
    s_exp = jnp.broadcast_to(jnp.exp(SOFT_CAP * s_tanh), (OWN_ALL, 128))
    exps[0] = s_exp
    rows_t[0] = jnp.transpose(inter)
    rows_t[1] = jnp.transpose(own_all)

    def back_slot(i, carry):
        back_user(i - 2 * USERS)
        reduce_steps(i)
        return carry

    lax.fori_loop(2 * USERS, SLOTS, back_slot, 0)

    own_all = oc[...].reshape(OWN_ALL, WIDTH)
    parts = []
    for u in range(USERS):
        parts.append(acc[u, c1 * 8 + c2 * 2 + y_hi])
    pooled = dot_split(jnp.concatenate(parts, axis=0), value_weight[...])
    normed = pooled * lax.rsqrt(jnp.mean(pooled * pooled, axis=1, keepdims=True) + 1e-6)
    mixed = (normed * own_all).astype(BF16)
    t_hidden = gelu(dot(mixed, head_weight[...]))
    t_logit = SOFT_CAP * jnp.tanh(
        jnp.sum(t_hidden * head_vector[...], axis=1, keepdims=True) / SOFT_CAP
    )
    lane = lax.broadcasted_iota(jnp.int32, (OWN_ALL, 128), 1)
    sub = lax.broadcasted_iota(jnp.int32, (OWN_ALL, 128), 0)
    logits_out[...] = jnp.sum(
        jnp.where(lane == sub % OWN, jnp.broadcast_to(t_logit, (OWN_ALL, 128)), 0.0).reshape(
            USERS, OWN, 128
        ),
        axis=1,
    )

    result(0).start()

    t_exp = jnp.broadcast_to(jnp.exp(t_logit), (OWN_ALL, 128))
    exps[1] = t_exp

    def exchange(slots, count, me, peer, send_sem, recv_sem):
        def copy(k, to):
            return pltpu.make_async_remote_copy(
                src_ref=slots.at[me],
                dst_ref=slots.at[me],
                send_sem=send_sem.at[k],
                recv_sem=recv_sem.at[me],
                device_id=to,
                device_id_type=MESH,
            )

        def arrival(k):
            return pltpu.make_async_remote_copy(
                src_ref=slots.at[me],
                dst_ref=slots.at[k],
                send_sem=send_sem.at[k],
                recv_sem=recv_sem.at[k],
                device_id=peer(k),
                device_id_type=MESH,
            )

        def start():
            for d in range(1, count):
                k = (me + d) % count
                copy(k, peer(k)).start()

        def wait():
            for d in range(1, count):
                k = (me + d) % count
                arrival(k).wait_recv()
            for d in range(1, count):
                k = (me + d) % count
                copy(k, peer(k)).wait_send()

        return start, wait

    st1[place8, 0] = jnp.sum(exps[0].reshape(USERS, OWN, 128), axis=1)
    st1[place8, 1] = jnp.sum(t_exp.reshape(USERS, OWN, 128), axis=1)

    def more_back(first, last):
        def one(u, carry):
            back_user(u)
            return carry

        lax.fori_loop(first, last, one, 0)

    done = SLOTS - 2 * USERS
    start, wait = exchange(st1, 8, place8, peer8, st1_s, st1_r)
    start()
    more_back(done, (done + USERS) // 2)
    wait()
    st2[place16] = jnp.sum(st1[...], axis=0)
    start, wait = exchange(st2, 16, place16, peer16, st2_s, st2_r)
    start()
    more_back((done + USERS) // 2, USERS)
    wait()
    sums = jnp.sum(st2[...], axis=0)

    def wide(v):
        return jnp.broadcast_to(v[:, None, :], (USERS, OWN, 128)).reshape(OWN_ALL, 128)

    scale = math.sqrt(4 * CAND_DEV / USERS)
    logit_grad = scale * (exps[0] / wide(sums[0]) - exps[1] / wide(sums[1]))
    row_scale[:, :128] = logit_grad
    row_scale[:, 128:] = logit_grad
    cand_scale[...] = row_scale[...] * oc[...].reshape(OWN_ALL, WIDTH)
    dh[0] = dh[0] * row_scale[...]
    dh[1] = dh[1] * row_scale[...]

    def mlp_half(h, carry):
        mlp[h] = dot_split2(rows_t[h], dh[0])
        return carry

    lax.fori_loop(0, 2, mlp_half, 0)

    others = [(place16 + d) % 16 for d in range(1, 16)]

    def all_reduce(n, gb, r0, r1, r2, out):
        def swap():
            return pltpu.make_async_remote_copy(
                src_ref=gb.at[1 - core],
                dst_ref=r0,
                send_sem=a0_s.at[n],
                recv_sem=a0_r.at[n],
                device_id=sibling,
                device_id_type=MESH,
            )

        def scatter(k, slot):
            return pltpu.make_async_remote_copy(
                src_ref=r0.at[k],
                dst_ref=r1.at[slot],
                send_sem=a1_s.at[n, k],
                recv_sem=a1_r.at[n, slot],
                device_id=peer16(k),
                device_id_type=MESH,
            )

        def spread(k, slot):
            return pltpu.make_async_remote_copy(
                src_ref=out.at[core, slot],
                dst_ref=out.at[core, slot],
                send_sem=a3_s.at[n, k],
                recv_sem=a3_r.at[n, slot],
                device_id=peer16(k),
                device_id_type=MESH,
            )

        def last(slot):
            return pltpu.make_async_remote_copy(
                src_ref=out.at[core],
                dst_ref=out.at[slot],
                send_sem=a4_s.at[n],
                recv_sem=a4_r.at[n],
                device_id=sibling,
                device_id_type=MESH,
            )

        start_y, wait_y = exchange(r2, 4, y, peer_y, a2_s.at[n], a2_r.at[n])

        def step0():
            swap().start()

        def step1():
            swap().wait()
            r0[...] = r0[...] + gb[core]
            for k in others:
                scatter(k, place16).start()
            r1[place16] = r0[place16]

        def step2():
            for k in others:
                scatter(k, k).wait_recv()
            r2[y] = jnp.sum(r1[...], axis=0)
            start_y()

        def step3():
            wait_y()
            out[core, place16] = jnp.sum(r2[...], axis=0)
            for k in others:
                spread(k, place16).start()

        def step4():
            for k in others:
                spread(k, k).wait_recv()
            last(core).start()

        def step5():
            for k in others:
                scatter(k, place16).wait_send()
                spread(k, place16).wait_send()
            last(core).wait_send()
            last(1 - core).wait_recv()

        return step0, step1, step2, step3, step4, step5

    first = all_reduce(0, gb0, r00, r10, r20, mlp_out)
    second = all_reduce(1, gb1, r01, r11, r21, att_out)
    for h in range(2):
        gb0[h] = mlp[h].reshape(16, 16, WIDTH)
    first[0]()

    for ab in range(2):
        rows = slice(ab * 64, ab * 64 + 64)

        def add(i, carry):
            p, e = carry
            for j in range(OWN):
                g = pre[i, j, rows, :]
                p = p + g * cand_scale[pl.ds(i * OWN + j, 1), :]
                e = e + g * row_scale[pl.ds(i * OWN + j, 1), :]
            return p, e

        zero = jnp.zeros((64, WIDTH), F32)
        p, e = lax.fori_loop(0, USERS, add, (zero, zero))
        gb1[0, ab * 8 : ab * 8 + 8] = p.reshape(8, 8, WIDTH)
        gb1[1, ab * 8 : ab * 8 + 8] = e.reshape(8, 8, WIDTH)
        if ab == 0:
            first[1]()
    second[0]()
    lane = lax.broadcasted_iota(jnp.int32, (OWN_ALL, 128), 1)
    sub = lax.broadcasted_iota(jnp.int32, (OWN_ALL, 128), 0)
    scale_row = diag_row(row_scale[:, :128])
    g_row = diag_row(jnp.sum(unit_sums[...] * scale_row, axis=1, keepdims=True))
    sm1[place8] = jnp.concatenate(
        [
            jnp.concatenate([g_row, jnp.zeros_like(g_row)], axis=1),
            jnp.sum(dh[0], axis=0, keepdims=True),
            jnp.sum(dh[1], axis=0, keepdims=True),
            jnp.zeros((5, WIDTH), F32),
        ],
        axis=0,
    )
    start, wait = exchange(sm1, 8, place8, peer8, sm1_s, sm1_r)
    start()
    second[1]()
    first[2]()
    wait()
    sm2[place16] = jnp.sum(sm1[...], axis=0)
    start, wait = exchange(sm2, 16, place16, peer16, sm2_s, sm2_r)
    start()
    second[2]()
    first[3]()
    second[3]()
    wait()
    small_out[...] = jnp.sum(sm2[...], axis=0)
    result(3).start()
    first[4]()
    second[4]()
    first[5]()
    result(1).start()
    second[5]()
    result(2).start()
    for k in range(4):
        result(k).wait()


def finish_kernel(
    logits,
    mlp,
    att,
    small,
    pair_weight,
    event_weight,
    scoring_bias,
    weigher,
    logits_out,
    pair_out,
    event_out,
    scoring_out,
    weigher_out,
    pooling_out,
    itemwise_out,
    hidden_out,
    output_out,
    logits_v,
    pair_v,
    event_v,
    scoring_v,
    weigher_v,
    hidden_v,
    output_v,
    out_sem,
):
    outputs = (
        (mlp.at[0], pooling_out),
        (mlp.at[1], itemwise_out),
        (pair_v, pair_out),
        (event_v, event_out),
        (scoring_v, scoring_out),
        (weigher_v, weigher_out),
        (hidden_v, hidden_out),
        (output_v, output_out),
        (logits_v, logits_out),
    )

    def give(k):
        return pltpu.make_async_copy(outputs[k][0], outputs[k][1], out_sem.at[k])

    for k in range(2):
        give(k).start()
    w = weigher[...]
    pair = jnp.transpose(att[:128])
    event = jnp.transpose(att[128:])
    pair_v[...] = pair * w
    event_v[...] = event * w
    give(2).start()
    give(3).start()
    g = small[0:1, :128]
    scoring_v[...] = g * w
    weigher_v[...] = scoring_bias[...] * g + jnp.sum(
        pair * pair_weight[...] + event * event_weight[...], axis=0, keepdims=True
    )
    hidden_v[...] = small[1:2, :]
    output_v[...] = small[2:3, :]
    logits_v[...] = logits[:, :OWN]
    for k in range(4, 9):
        give(k).start()
    for k in range(9):
        give(k).wait()


def body(
    history,
    candidates,
    short_hist,
    lengths,
    pad_mask,
    short_mask,
    query_gain,
    value_weight,
    head_weight,
    head_vector,
    pair_weight,
    event_weight,
    scoring_bias,
    weigher,
    pooling_weight,
    itemwise_weight,
    hidden_bias,
    output_vector,
):
    vmem = pl.BlockSpec(memory_space=pltpu.VMEM)
    row = lambda v: v.reshape(1, -1)
    dma = pltpu.SemaphoreType.DMA
    logits, mlp, att, small = pl.pallas_call(
        main_kernel,
        out_shape=(
            jax.ShapeDtypeStruct((USERS, 128), F32),
            jax.ShapeDtypeStruct((2, 16, 16, WIDTH), F32),
            jax.ShapeDtypeStruct((2, 16, 8, WIDTH), F32),
            jax.ShapeDtypeStruct((8, WIDTH), F32),
        ),
        in_specs=[
            pl.BlockSpec(memory_space=pltpu.SMEM),
        ]
        + [pl.BlockSpec(memory_space=pl.ANY)] * 17,
        out_specs=(pl.BlockSpec(memory_space=pl.ANY),) * 4,
        scratch_shapes=[
            pltpu.VMEM((USERS, EVENTS), jnp.int32),
            pltpu.VMEM((USERS, SHORT), jnp.int32),
            pltpu.VMEM((1, WIDTH), F32),
            pltpu.VMEM((1, WIDTH), F32),
            pltpu.VMEM((1, SCORE_H), F32),
            pltpu.VMEM((1, SCORE_H), F32),
            pltpu.VMEM((1, WIDTH), F32),
            pltpu.VMEM((1, WIDTH), F32),
            pltpu.VMEM((USERS, 128), F32),
            pltpu.VMEM((2, 16, 16, WIDTH), F32),
            pltpu.VMEM((2, 16, 8, WIDTH), F32),
            pltpu.VMEM((8, WIDTH), F32),
            pltpu.VMEM((USERS, EVENTS, WIDTH), BF16),
            pltpu.VMEM((USERS, CAND_DEV, WIDTH), BF16),
            pltpu.VMEM((USERS, SHORT, WIDTH), BF16),
            pltpu.VMEM((WIDTH, WIDTH), BF16),
            pltpu.VMEM((WIDTH, WIDTH), BF16),
            pltpu.VMEM((WIDTH, SCORE_H), F32),
            pltpu.VMEM((WIDTH, SCORE_H), F32),
            pltpu.VMEM((WIDTH, WIDTH), F32),
            pltpu.VMEM((WIDTH, WIDTH), F32),
            pltpu.VMEM((CAND_DEV, WIDTH), BF16),
            pltpu.VMEM((CAND_DEV, EVENTS), F32),
            pltpu.VMEM((CAND_DEV, EVENTS), BF16),
            pltpu.VMEM((CAND_DEV, 128), F32),
            pltpu.VMEM((CAND_DEV, 128), F32),
            pltpu.VMEM((CAND_DEV, 128), F32),
            pltpu.VMEM((CAND_DEV, 128), F32),
            pltpu.VMEM((CAND_DEV, 128), F32),
            pltpu.VMEM((USERS, BLOCKS, OWN, WIDTH), F32),
            pltpu.VMEM((3, USERS, 4, 8, 128), F32),
            pltpu.VMEM((USERS, 3, 8, OWN, WIDTH), F32),
            pltpu.VMEM((USERS, 3, 2, OWN, WIDTH), F32),
            pltpu.VMEM((USERS, 1, 1, OWN, WIDTH), F32),
            pltpu.VMEM((USERS, 7, 8, 128), F32),
            pltpu.VMEM((USERS, OWN, WIDTH), F32),
            pltpu.VMEM((SCORE_H, WIDTH), F32),
            pltpu.VMEM((SCORE_H, WIDTH), F32),
            pltpu.VMEM((SCORE_H, WIDTH), F32),
            pltpu.VMEM((SCORE_H, WIDTH), F32),
            pltpu.VMEM((OWN // CGROUP, 2, CGROUP * SCORE_H, WIDTH), BF16),
            pltpu.VMEM((USERS, OWN, SCORE_H, SHORT), F32),
            pltpu.VMEM((USERS, OWN, SHORT), F32),
            pltpu.VMEM((USERS, OWN, WIDTH), F32),
            pltpu.VMEM((USERS, OWN, WIDTH), F32),
            pltpu.VMEM((OWN, SHORT), F32),
            pltpu.VMEM((2, OWN_ALL, 128), F32),
            pltpu.VMEM((SCORE_H, OWN_ALL), F32),
            pltpu.VMEM((OWN_ALL, WIDTH), F32),
            pltpu.VMEM((OWN_ALL, WIDTH), F32),
            pltpu.VMEM((2, WIDTH, OWN_ALL), F32),
            pltpu.VMEM((2, OWN_ALL, WIDTH), F32),
            pltpu.VMEM((2, WIDTH, WIDTH), F32),
            pltpu.VMEM((8, 2, USERS, 128), F32),
            pltpu.VMEM((16, 2, USERS, 128), F32),
            pltpu.VMEM((8, 8, WIDTH), F32),
            pltpu.VMEM((16, 8, WIDTH), F32),
            pltpu.VMEM((2, 16, 16, WIDTH), F32),
            pltpu.VMEM((2, 16, 8, WIDTH), F32),
            pltpu.VMEM((16, 16, WIDTH), F32),
            pltpu.VMEM((16, 8, WIDTH), F32),
            pltpu.VMEM((16, 16, WIDTH), F32),
            pltpu.VMEM((16, 8, WIDTH), F32),
            pltpu.VMEM((4, 16, WIDTH), F32),
            pltpu.VMEM((4, 8, WIDTH), F32),
            dma((USERS,)),
            dma((USERS,)),
            dma((13,)),
            dma((2,)),
            dma((4,)),
            dma((3, USERS, 3)),
            dma((3, USERS, 3)),
            dma((3, USERS, 3)),
            dma((3, USERS, 3)),
            dma((8,)),
            dma((8,)),
            dma((16,)),
            dma((16,)),
            dma((8,)),
            dma((8,)),
            dma((16,)),
            dma((16,)),
            dma((2,)),
            dma((2,)),
            dma((2, 16)),
            dma((2, 16)),
            dma((2, 4)),
            dma((2, 4)),
            dma((2, 16)),
            dma((2, 16)),
            dma((2,)),
            dma((2,)),
        ],
        compiler_params=pltpu.CompilerParams(
            collective_id=0, has_side_effects=True, vmem_limit_bytes=62 * 1024 * 1024
        ),
        name="main_kernel",
    )(
        lengths,
        history,
        candidates,
        short_hist,
        value_weight,
        head_weight,
        pair_weight,
        event_weight,
        pooling_weight,
        itemwise_weight,
        pad_mask,
        short_mask,
        row(query_gain),
        row(head_vector),
        row(scoring_bias),
        row(weigher),
        row(hidden_bias),
        row(output_vector),
    )
    out = pl.pallas_call(
        finish_kernel,
        out_shape=(
            jax.ShapeDtypeStruct((USERS, OWN), F32),
            jax.ShapeDtypeStruct((WIDTH, SCORE_H), F32),
            jax.ShapeDtypeStruct((WIDTH, SCORE_H), F32),
            jax.ShapeDtypeStruct((1, SCORE_H), F32),
            jax.ShapeDtypeStruct((1, SCORE_H), F32),
            jax.ShapeDtypeStruct((WIDTH, WIDTH), F32),
            jax.ShapeDtypeStruct((WIDTH, WIDTH), F32),
            jax.ShapeDtypeStruct((1, WIDTH), F32),
            jax.ShapeDtypeStruct((1, WIDTH), F32),
        ),
        in_specs=[vmem] * 8,
        out_specs=(pl.BlockSpec(memory_space=pl.ANY),) * 9,
        scratch_shapes=[
            pltpu.VMEM((USERS, OWN), F32),
            pltpu.VMEM((WIDTH, SCORE_H), F32),
            pltpu.VMEM((WIDTH, SCORE_H), F32),
            pltpu.VMEM((1, SCORE_H), F32),
            pltpu.VMEM((1, SCORE_H), F32),
            pltpu.VMEM((1, WIDTH), F32),
            pltpu.VMEM((1, WIDTH), F32),
            dma((9,)),
        ],
        name="finish_kernel",
    )(logits, mlp.reshape(2, WIDTH, WIDTH), att.reshape(256, WIDTH), small, pair_weight, event_weight, row(scoring_bias), row(weigher))
    flat = lambda v: v.reshape(-1)
    return (
        out[0],
        out[1],
        out[2],
        flat(out[3]),
        flat(out[4]),
        out[5],
        out[6],
        flat(out[7]),
        flat(out[8]),
    )


def solution(mesh):
    placed = (P(None, "ctx", None), P(None, "cand", None), P(), P(), P(None, "ctx")) + (P(),) * 13
    return jax.shard_map(
        body,
        mesh=mesh,
        in_specs=placed,
        out_specs=(P(None, ("cand", "ctx")),) + (P(),) * 8,
        check_vma=False,
    )
```
